32 devices in a mesh: blk: 8 (over z, y), seq: 4 (over x, core).
Axes of the slice: x: 2, y: 2, z: 4, core: 2. Of those that a mesh axis runs over, the one named last changes fastest.
Arguments:
- tokens: bfloat16 [3072, 4096], P('seq', 'blk'), may hold values from -6 to 6
- grad_out: bfloat16 [3072, 4096], P('seq', 'blk'), may hold values from -0.109375 to 0.109375
- input_weight_blocks: bfloat16 [1024, 128, 128], P('blk'), may hold values from -0.25 to 0.25
- output_weight_blocks: bfloat16 [1024, 128, 128], P('blk'), may hold values from -0.25 to 0.25
- row_ids: int32 [1024], P('blk'), may hold values from 0 to 31, as said below
- lengths: int32 [4], P('seq'), may hold values from 1 to 768, 1920 in all
Outputs:
- grad_in: bfloat16 [1024, 128, 128], P('blk', 'seq')
- grad_w_out: bfloat16 [1024, 128, 128], P('blk', 'seq')
The draws below stay inside these ranges and needn't reach their ends.
Inputs may be any that keep to these rules, and one draw needn't show every extreme that they name: `row_ids`: the 4 blocks of each hidden column block have distinct row blocks. `lengths`: some window is full.
All inputs are finite; a program needn't handle non-finite values. No bound on the sum of `lengths` on one device may be relied on, other than what follows from the above.
Results may differ from the reference program's by a relative error of at most 0.015.
Values may be sent and summed in bfloat16 or wider, within the bound.
A program may use at most 128 MiB of HBM per device.

```python
import math
import jax
import jax.numpy as jnp
import numpy as np
from jax import lax

D = 4096
BLOCK_SIDE = 128
TP = 768
RB = 32
CB = 256
BLOCKS_PER_COLUMN = 4
SLOT_COUNT = 1024
TOKENS = 3072
N_SEQ = 4


def draw_row_ids(key, part):
    base_key = jax.random.fold_in(key, 11)
    row_order = jax.random.permutation(jax.random.fold_in(base_key, 1), RB)
    col_order = jax.random.permutation(jax.random.fold_in(base_key, 2), CB)
    offset_draw = jax.random.randint(jax.random.fold_in(base_key, 3), (), 0, RB)
    anchors = (col_order + offset_draw) % RB
    powers = jnp.left_shift(jnp.ones((BLOCKS_PER_COLUMN - 1,), jnp.int32), jnp.arange(BLOCKS_PER_COLUMN - 1, dtype=jnp.int32))
    offsets = jnp.concatenate([jnp.zeros((1,), jnp.int32), powers])
    picks = jnp.bitwise_xor(anchors[:, None].astype(jnp.int32), offsets[None, :])
    return row_order[picks].reshape(-1).astype(jnp.int32)


def level_of(own_key, shape, cuts, smallest, top_value):
    factor_of, own = 1.0, jax.random.fold_in(own_key, 6)
    for axis_at, blocks in cuts:
        heights = jnp.exp(jax.random.uniform(jax.random.fold_in(own, axis_at), (blocks,), jnp.float32, smallest / len(cuts), top_value / len(cuts)))
        factor_of = factor_of * jnp.repeat(heights, shape[axis_at] // blocks).reshape([-1 if axis == axis_at else 1 for axis in range(len(shape))])
    return factor_of


def split_up(number_of, total, bound, lean):
    weights = [(1 << 20) // math.isqrt(rank ** lean) + 1 for rank in range(2, number_of + 1)]
    surplus, holding = total - bound - (number_of - 1), [1] * (number_of - 1)
    while surplus > 0:
        movable = [i for i in range(number_of - 1) if holding[i] < bound]
        mass, remaining = sum([weights[i] for i in movable]), surplus
        for i in movable:
            extra = min(bound - holding[i], max(1, remaining * weights[i] // mass), surplus)
            holding[i] = holding[i] + extra
            surplus = surplus - extra
    return np.array([bound] + holding)


def ragged(stream_key, number_of, total, limit, slope):
    if number_of == 2:
        one = jax.random.randint(stream_key, (), max(1, total - limit), min(limit, total - 1) + 1)
        return jnp.stack([one, total - one])
    tallies = jnp.asarray(split_up(number_of, total, limit, slope), jnp.int32)
    pairs = (number_of - 1) // 2
    donor, receiver = tallies[1:1 + 2 * pairs:2], tallies[2:2 + 2 * pairs:2]
    slack = jnp.minimum(donor - 1, limit - receiver)
    passed = jax.random.randint(jax.random.fold_in(stream_key, 1), (pairs,), 0, 1 << 20) % (slack + 1)
    tallies = tallies.at[1:1 + 2 * pairs:2].set(donor - passed).at[2:2 + 2 * pairs:2].set(receiver + passed)
    return tallies[jax.random.permutation(jax.random.fold_in(stream_key, 2), number_of)]


def gaussian(stream_key, dims, spread, bound, shards=(), kind=jnp.bfloat16):
    values = jax.random.normal(stream_key, dims, jnp.float32) * spread
    if len(shards) > 0:
        values = level_of(stream_key, dims, shards, -0.22, 0.18) * values
    return jnp.clip(values, min=-bound, max=bound).astype(kind)


def setup_inputs(seed: int = 0) -> dict:
    splits = jax.random.split(jax.random.key(seed), 7)
    return {
        "tokens": gaussian(splits[0], (TOKENS, D), 1.0, 6.0, ((0, 4), (1, 8))),
        "grad_out": gaussian(splits[1], (TOKENS, D), TOKENS ** -0.5, 0.109375, ((0, 4), (1, 8))),
        "input_weight_blocks": gaussian(splits[2], (SLOT_COUNT, BLOCK_SIDE, BLOCK_SIDE), (BLOCKS_PER_COLUMN * BLOCK_SIDE) ** -0.5, 0.25, ((0, 8),)),
        "output_weight_blocks": gaussian(splits[3], (SLOT_COUNT, BLOCK_SIDE, BLOCK_SIDE), (BLOCKS_PER_COLUMN * BLOCK_SIDE) ** -0.5, 0.25, ((0, 8),)),
        "row_ids": draw_row_ids(jax.random.fold_in(splits[6], 71), 0),
        "lengths": ragged(splits[5], N_SEQ, N_SEQ * TP * 5 // 8, TP, 2).astype(jnp.int32),
    }


gelu_scale = 0.7978845608


def gelu_pair(pre_act):
    tanh_val = jnp.tanh(gelu_scale * (pre_act + 0.044715 * pre_act * pre_act * pre_act))
    activation = 0.5 * pre_act * (1.0 + tanh_val)
    gelu_slope = 0.5 * (1.0 + tanh_val) + 0.5 * pre_act * (1.0 - tanh_val * tanh_val) * gelu_scale * (1.0 + 0.134145 * pre_act * pre_act)
    return activation, gelu_slope


def reference(tokens, grad_out, input_weight_blocks, output_weight_blocks, row_ids, lengths):
    live_rows = lax.iota(jnp.int32, TP)[None, :] < lengths[:, None]
    x_panels = tokens.reshape(N_SEQ, TP, RB, BLOCK_SIDE)
    g_panels = grad_out.reshape(N_SEQ, TP, RB, BLOCK_SIDE)
    masked = jnp.where(live_rows[:, :, None, None], g_panels, jnp.zeros_like(g_panels)).astype(jnp.bfloat16)
    w_in_f = input_weight_blocks.astype(jnp.float32)
    output_weight_flat = output_weight_blocks.astype(jnp.float32)

    def window_step(totals, panel_pair):
        x_panel, g_panel = panel_pair
        x_slots = x_panel[:, row_ids, :].astype(jnp.float32)
        gradient_slots = g_panel[:, row_ids, :].astype(jnp.float32)
        pre_slot = jnp.einsum("tkc,kch->tkh", x_slots, w_in_f)
        pre_act = pre_slot.reshape(TP, CB, BLOCKS_PER_COLUMN, BLOCK_SIDE).sum(2)
        activation, gelu_slope = gelu_pair(pre_act)
        activation = activation.astype(jnp.bfloat16)
        slot_gradient = jnp.einsum("xcn,cpn->xcp", gradient_slots, output_weight_flat)
        grad_act = slot_gradient.reshape(TP, CB, BLOCKS_PER_COLUMN, BLOCK_SIDE).sum(2)
        grad_pre = (grad_act * gelu_slope).astype(jnp.bfloat16)
        x_four = x_slots.reshape(TP, CB, BLOCKS_PER_COLUMN, BLOCK_SIDE)
        g_four = gradient_slots.reshape(TP, CB, BLOCKS_PER_COLUMN, BLOCK_SIDE)
        input_share = jnp.einsum("tgrc,tgh->grch", x_four, grad_pre.astype(jnp.float32))
        output_share = jnp.einsum("tgh,tgrf->grhf", activation.astype(jnp.float32), g_four)
        input_share = input_share.reshape(SLOT_COUNT, BLOCK_SIDE, BLOCK_SIDE).astype(jnp.bfloat16).astype(jnp.float32)
        output_share = output_share.reshape(SLOT_COUNT, BLOCK_SIDE, BLOCK_SIDE).astype(jnp.bfloat16).astype(jnp.float32)
        return (totals[0] + input_share, totals[1] + output_share), None

    empty_weight_block = jnp.zeros((SLOT_COUNT, BLOCK_SIDE, BLOCK_SIDE), jnp.float32)
    totals, unused = lax.scan(window_step, (empty_weight_block, empty_weight_block), (x_panels, masked))
    return totals[0].astype(jnp.bfloat16), totals[1].astype(jnp.bfloat16)
```

```python
import jax
import jax.numpy as jnp
from jax import lax
from jax.experimental import pallas as pl
from jax.experimental.pallas import tpu as pltpu
from jax.sharding import PartitionSpec as P

BLOCK_SIDE = 128
BLOCKS_PER_COLUMN = 4


gelu_scale = 0.7978845608


def gelu_pair(pre_act):
    tanh_val = jnp.tanh(gelu_scale * (pre_act + 0.044715 * pre_act * pre_act * pre_act))
    activation = 0.5 * pre_act * (1.0 + tanh_val)
    gelu_slope = 0.5 * (1.0 + tanh_val) + 0.5 * pre_act * (
        1.0 - tanh_val * tanh_val
    ) * gelu_scale * (1.0 + 0.134145 * pre_act * pre_act)
    return (activation, gelu_slope)


def shards(tokens, grad_out, input_weight_blocks, output_weight_blocks, row_ids, lengths):
    tok_rows = tokens.shape[0]
    groups = input_weight_blocks.shape[0] // BLOCKS_PER_COLUMN
    live_rows = lax.iota(jnp.int32, tok_rows)[:, None] < lengths[0]
    masked = jnp.where(live_rows, grad_out, jnp.zeros_like(grad_out))
    features = lax.all_gather(tokens, "blk", axis=1, tiled=True)
    x_slots = features.reshape(tok_rows, -1, BLOCK_SIDE)[:, row_ids, :]
    pre_slot = jnp.einsum(
        "tkc,kch->tkh", x_slots, input_weight_blocks, preferred_element_type=jnp.float32
    )
    pre_act = pre_slot.reshape(tok_rows, groups, BLOCKS_PER_COLUMN, BLOCK_SIDE).sum(2)
    activation, gelu_slope = gelu_pair(pre_act)
    activation = activation.astype(jnp.bfloat16)
    gradient = lax.all_gather(masked, "blk", axis=1, tiled=True)
    gradient_slots = gradient.reshape(tok_rows, -1, BLOCK_SIDE)[:, row_ids, :]
    g_four = gradient_slots.reshape(tok_rows, groups, BLOCKS_PER_COLUMN, BLOCK_SIDE)
    output_share = jnp.einsum(
        "tgh,tgrf->grhf", activation, g_four, preferred_element_type=jnp.float32
    )
    output_share = output_share.reshape(-1, BLOCK_SIDE, BLOCK_SIDE)
    slot_gradient = jnp.einsum(
        "xcn,cpn->xcp", gradient_slots, output_weight_blocks, preferred_element_type=jnp.float32
    )
    grad_act = slot_gradient.reshape(tok_rows, groups, BLOCKS_PER_COLUMN, BLOCK_SIDE).sum(2)
    grad_pre = (grad_act * gelu_slope).astype(jnp.bfloat16)
    x_four = x_slots.reshape(tok_rows, groups, BLOCKS_PER_COLUMN, BLOCK_SIDE)
    input_share = jnp.einsum("tgrc,tgh->grch", x_four, grad_pre, preferred_element_type=jnp.float32)
    input_share = input_share.reshape(-1, BLOCK_SIDE, BLOCK_SIDE)
    in_total, out_total = (
        lax.psum_scatter(
            input_share.astype(jnp.bfloat16), "seq", scatter_dimension=1, tiled=True
        ).astype(jnp.float32),
        lax.psum_scatter(
            output_share.astype(jnp.bfloat16), "seq", scatter_dimension=1, tiled=True
        ).astype(jnp.float32),
    )
    return (in_total.astype(jnp.bfloat16), out_total.astype(jnp.bfloat16))


PLAN_MESH = (8, 4)
NZ = 4
MESH = pl.DeviceIdType.MESH


def pack_gather_grad_kernel(
    tokens_ref, grad_ref, w_in_ref, w_out_ref, ids_ref, len_ref, out_in_ref, out_out_ref,
    chip, lens, give, got, feat, w_in, w_out, part, from_core, to_x, from_x,
    load_sem, core_send, core_recv, x_send, x_recv, z_send, z_recv, y_send, y_recv,
    sum_core_send, sum_core_recv, sum_x_send, sum_x_recv,
):
    rows = chip.shape[2]
    width = chip.shape[3]
    keep = feat.shape[1]
    spare = got.shape[1]
    per = width // BLOCK_SIDE
    n_rows = feat.shape[0] // 2
    groups = part.shape[0]
    pieces = 2 * per

    blk = lax.axis_index("blk")
    seq = lax.axis_index("seq")
    z, y = blk // 2, blk % 2
    x, core = seq // 2, seq % 2
    core_dev = {"seq": seq + 1 - 2 * core}
    x_dev = {"seq": seq + 2 - 4 * x}
    y_dev = {"blk": blk + 1 - 2 * y}
    up_dev = {"blk": blk + 2}
    down_dev = {"blk": blk - 2}

    def remote(src, dst, send, recv, device):
        return pltpu.make_async_remote_copy(
            src_ref=src, dst_ref=dst, send_sem=send, recv_sem=recv,
            device_id=device, device_id_type=MESH,
        )

    barrier = pltpu.get_barrier_semaphore()
    for device in (core_dev, x_dev, y_dev):
        pl.semaphore_signal(barrier, inc=1, device_id=device, device_id_type=MESH)

    @pl.when(z > 0)
    def _():
        pl.semaphore_signal(barrier, inc=1, device_id=down_dev, device_id_type=MESH)

    @pl.when(z < NZ - 1)
    def _():
        pl.semaphore_signal(barrier, inc=1, device_id=up_dev, device_id_type=MESH)

    own_loads = [
        pltpu.make_async_copy(ref, chip.at[a, core], load_sem.at[a])
        for a, ref in enumerate((tokens_ref, grad_ref))
    ]
    weight_loads = [
        pltpu.make_async_copy(w_in_ref, w_in, load_sem.at[2]),
        pltpu.make_async_copy(w_out_ref, w_out, load_sem.at[3]),
    ]
    for load in own_loads:
        load.start()
    lens[core] = jnp.full(lens.shape[1:], len_ref[0], jnp.int32)
    pl.semaphore_wait(barrier, 3 + jnp.where(z > 0, 1, 0) + jnp.where(z < NZ - 1, 1, 0))

    len_swap = remote(lens.at[core], lens.at[core], core_send.at[2], core_recv.at[2], core_dev)
    len_swap.start()
    swaps = [
        remote(ref, chip.at[a, core], core_send.at[a], core_recv.at[a], core_dev)
        for a, ref in enumerate((tokens_ref, grad_ref))
    ]
    for swap in swaps:
        swap.start()
    for load in weight_loads:
        load.start()
    len_swap.wait()
    len_a = lens[0][0:1, 0:1]
    len_b = lens[1][0:1, 0:1]
    count = len_a + len_b
    row = lax.broadcasted_iota(jnp.int32, (1, 2 * rows), 1)
    place = jnp.where(
        row < rows,
        jnp.where(row < len_a, row, -1),
        jnp.where(row - rows < len_b, row - rows + len_a, -1),
    )
    odd_give = jnp.bitwise_and(4 * keep - count + core, 1)
    odd_got = jnp.bitwise_and(count + core, 1)
    keep_at = 2 * lax.broadcasted_iota(jnp.int32, (keep, 1), 0) + core
    give_at = 2 * keep + odd_give + 2 * lax.broadcasted_iota(jnp.int32, (spare, 1), 0)
    got_at = count + odd_got + 2 * lax.broadcasted_iota(jnp.int32, (1, spare), 1)
    one, zero = jnp.float32(1), jnp.float32(0)
    pick_keep = jnp.where(place == keep_at, one, zero).astype(jnp.bfloat16)
    pick_give = jnp.where(place == give_at, one, zero).astype(jnp.bfloat16)
    pick_got = jnp.where(got_at == keep_at, one, zero).astype(jnp.bfloat16)

    def piece_at(a, source, i):
        return a * n_rows + per * source + i

    def feat_piece(source, p):
        return feat.at[(p // per) * n_rows + per * source + p % per]

    def z_copy(up, source_z, p, recv_only=False):
        ref = feat_piece(2 * source_z + y, p)
        return remote(
            ref, ref, z_send.at[0 if up else 1, source_z, p], z_recv.at[source_z, p],
            y_dev if recv_only else (up_dev if up else down_dev),
        )

    def y_copy(source_z, source_y, p):
        ref = feat_piece(2 * source_z + source_y, p)
        return remote(ref, ref, y_send.at[source_z, p], y_recv.at[source_z, p], y_dev)

    def both(a):
        return chip[a].reshape(2 * rows, width)

    x_moves = []
    for a in range(2):
        own_loads[a].wait()
        swaps[a].wait()
        give[a] = jnp.dot(pick_give, both(a), preferred_element_type=jnp.float32).astype(jnp.bfloat16)
        move = remote(give.at[a], got.at[a], x_send.at[a], x_recv.at[a], x_dev)
        move.start()
        x_moves.append(move)
    kept = [jnp.dot(pick_keep, both(a), preferred_element_type=jnp.float32) for a in range(2)]
    for a in range(2):
        x_moves[a].wait()
        block = kept[a] + jnp.dot(pick_got, got[a], preferred_element_type=jnp.float32)
        block = block.astype(jnp.bfloat16)
        for i in range(per):
            feat[piece_at(a, blk, i)] = block[:, i * BLOCK_SIDE : (i + 1) * BLOCK_SIDE]

        def send_own(i, carry):
            p = a * per + i
            y_copy(z, y, p).start()

            @pl.when(z < NZ - 1)
            def _():
                z_copy(True, z, p).start()

            @pl.when(z > 0)
            def _():
                z_copy(False, z, p).start()

            return carry

        lax.fori_loop(0, per, send_own, 0)

    for step in range(NZ - 1):

        def pass_on(p, carry):
            below = z - 1 - step
            above = z + 1 + step

            @pl.when(below >= 0)
            def _():
                z_copy(True, below, p, recv_only=True).wait_recv()
                y_copy(below, y, p).start()

                @pl.when(z < NZ - 1)
                def _():
                    z_copy(True, below, p).start()

            @pl.when(above < NZ)
            def _():
                z_copy(False, above, p, recv_only=True).wait_recv()
                y_copy(above, y, p).start()

                @pl.when(z > 0)
                def _():
                    z_copy(False, above, p).start()

            return carry

        lax.fori_loop(0, pieces, pass_on, 0)

    def end_gather(p, carry):
        for source_z in range(NZ):
            y_copy(source_z, 1 - y, p).wait_recv()
        return carry

    lax.fori_loop(0, pieces, end_gather, 0)

    for load in weight_loads:
        load.wait()

    def core_sum(g):
        return remote(part.at[g, 1 - core], from_core.at[g], sum_core_send.at[g], sum_core_recv.at[g], core_dev)

    def x_sum(g):
        return remote(to_x.at[g], from_x.at[g], sum_x_send.at[g], sum_x_recv.at[g], x_dev)

    def send_sum(g):
        core_sum(g).wait_recv()
        total = part[g, core, 1 - x].astype(jnp.float32) + from_core[g, 1 - x].astype(jnp.float32)
        to_x[g] = total.astype(jnp.bfloat16)
        x_sum(g).start()

    quarter = BLOCK_SIDE // 4

    def group(g, carry):
        ids = [ids_ref[BLOCKS_PER_COLUMN * g + i] for i in range(BLOCKS_PER_COLUMN)]
        x_cat = jnp.concatenate([feat[r] for r in ids], axis=1)
        g_cat = jnp.concatenate([feat[n_rows + r] for r in ids], axis=1)
        slots = pl.ds(BLOCKS_PER_COLUMN * g, BLOCKS_PER_COLUMN)
        w_rows = w_in[slots].reshape(BLOCKS_PER_COLUMN * BLOCK_SIDE, BLOCK_SIDE)
        wo = w_out[slots]
        w_cols = jnp.concatenate([wo[i] for i in range(BLOCKS_PER_COLUMN)], axis=1)
        pre_act = jnp.dot(x_cat, w_rows, preferred_element_type=jnp.float32)
        grad_act = lax.dot_general(
            g_cat, w_cols, (((1,), (1,)), ((), ())), preferred_element_type=jnp.float32
        )
        activation, gelu_slope = gelu_pair(pre_act)
        activation = activation.astype(jnp.bfloat16)
        grad_pre = (grad_act * gelu_slope).astype(jnp.bfloat16)
        first = (((0,), (0,)), ((), ()))
        share_in = lax.dot_general(grad_pre, x_cat, first, preferred_element_type=jnp.float32)
        share_out = lax.dot_general(activation, g_cat, first, preferred_element_type=jnp.float32)
        for i in range(BLOCKS_PER_COLUMN):
            cols = slice(i * BLOCK_SIDE, (i + 1) * BLOCK_SIDE)
            two = (share_in[:, cols].T, share_out[:, cols])
            for a in range(2):
                rounded = two[a].astype(jnp.bfloat16)
                for q in range(4):
                    part[g, q % 2, q // 2, a, i] = rounded[q * quarter : (q + 1) * quarter]
        core_sum(g).start()

        @pl.when(g > 0)
        def _():
            send_sum(g - 1)

        return carry

    lax.fori_loop(0, groups, group, 0)
    send_sum(groups - 1)

    def finish(g, carry):
        x_sum(g).wait_recv()
        total = (
            part[g, core, x].astype(jnp.float32)
            + from_core[g, x].astype(jnp.float32)
            + from_x[g].astype(jnp.float32)
        ).astype(jnp.bfloat16)
        slots = pl.ds(BLOCKS_PER_COLUMN * g, BLOCKS_PER_COLUMN)
        out_in_ref[slots] = total[0]
        out_out_ref[slots] = total[1]
        return carry

    lax.fori_loop(0, groups, finish, 0)

    def end_sums(g, carry):
        core_sum(g).wait_send()
        x_sum(g).wait_send()
        return carry

    lax.fori_loop(0, groups, end_sums, 0)

    def end_sends(p, carry):
        for source_z in range(NZ):
            y_copy(source_z, y, p).wait_send()

            @pl.when(jnp.logical_and(z < NZ - 1, source_z <= z))
            def _():
                z_copy(True, source_z, p).wait_send()

            @pl.when(jnp.logical_and(z > 0, source_z >= z))
            def _():
                z_copy(False, source_z, p).wait_send()

        return carry

    lax.fori_loop(0, pieces, end_sends, 0)


def packed_shards(tokens, grad_out, input_weight_blocks, output_weight_blocks, row_ids, lengths):
    rows, width = tokens.shape
    slots = input_weight_blocks.shape[0]
    groups = slots // BLOCKS_PER_COLUMN
    n_blk, n_seq = PLAN_MESH
    keep = rows * 5 // 8
    spare = rows - keep
    n_rows = n_blk * width // BLOCK_SIDE
    pieces = 2 * width // BLOCK_SIDE
    quarter = BLOCK_SIDE // n_seq
    sums = (2, BLOCKS_PER_COLUMN, quarter, BLOCK_SIDE)
    bf16 = jnp.bfloat16
    dma = pltpu.SemaphoreType.DMA
    any_spec = pl.BlockSpec(memory_space=pl.ANY)
    smem = pl.BlockSpec(memory_space=pltpu.SMEM)
    vmem = pl.BlockSpec(memory_space=pltpu.VMEM)
    out = jax.ShapeDtypeStruct((slots, quarter, BLOCK_SIDE), bf16)
    return pl.pallas_call(
        pack_gather_grad_kernel,
        out_shape=(out, out),
        in_specs=[any_spec] * 4 + [smem] * 2,
        out_specs=(vmem, vmem),
        scratch_shapes=[
            pltpu.VMEM((2, 2, rows, width), bf16),
            pltpu.VMEM((2, 8, 128), jnp.int32),
            pltpu.VMEM((2, spare, width), bf16),
            pltpu.VMEM((2, spare, width), bf16),
            pltpu.VMEM((2 * n_rows, keep, BLOCK_SIDE), bf16),
            pltpu.VMEM((slots, BLOCK_SIDE, BLOCK_SIDE), bf16),
            pltpu.VMEM((slots, BLOCK_SIDE, BLOCK_SIDE), bf16),
            pltpu.VMEM((groups, 2, 2) + sums, bf16),
            pltpu.VMEM((groups, 2) + sums, bf16),
            pltpu.VMEM((groups,) + sums, bf16),
            pltpu.VMEM((groups,) + sums, bf16),
            dma((4,)),
            dma((3,)),
            dma((3,)),
            dma((2,)),
            dma((2,)),
            dma((2, NZ, pieces)),
            dma((NZ, pieces)),
            dma((NZ, pieces)),
            dma((NZ, pieces)),
            dma((groups,)),
            dma((groups,)),
            dma((groups,)),
            dma((groups,)),
        ],
        compiler_params=pltpu.CompilerParams(
            collective_id=0, has_side_effects=True, vmem_limit_bytes=56 * 1024 * 1024
        ),
    )(tokens, grad_out, input_weight_blocks, output_weight_blocks, row_ids, lengths)


def solution(mesh):
    return jax.shard_map(
        packed_shards if tuple(mesh.shape.values()) == PLAN_MESH else shards,
        mesh=mesh,
        in_specs=(
            P("seq", "blk"),
            P("seq", "blk"),
            P("blk", None, None),
            P("blk", None, None),
            P("blk"),
            P("seq"),
        ),
        out_specs=(P("blk", "seq", None), P("blk", "seq", None)),
        check_vma=False,
    )
```

```python
import jax
import jax.numpy as jnp
from jax import lax
from jax.experimental import pallas as pl
from jax.experimental.pallas import tpu as pltpu
from jax.sharding import PartitionSpec as P

BLOCK_SIDE = 128
BLOCKS_PER_COLUMN = 4


gelu_scale = 0.7978845608


def gelu_pair(pre_act):
    tanh_val = jnp.tanh(gelu_scale * (pre_act + 0.044715 * pre_act * pre_act * pre_act))
    activation = 0.5 * pre_act * (1.0 + tanh_val)
    gelu_slope = 0.5 * (1.0 + tanh_val) + 0.5 * pre_act * (
        1.0 - tanh_val * tanh_val
    ) * gelu_scale * (1.0 + 0.134145 * pre_act * pre_act)
    return (activation, gelu_slope)


def shards(tokens, grad_out, input_weight_blocks, output_weight_blocks, row_ids, lengths):
    tok_rows = tokens.shape[0]
    groups = input_weight_blocks.shape[0] // BLOCKS_PER_COLUMN
    live_rows = lax.iota(jnp.int32, tok_rows)[:, None] < lengths[0]
    masked = jnp.where(live_rows, grad_out, jnp.zeros_like(grad_out))
    features = lax.all_gather(tokens, "blk", axis=1, tiled=True)
    x_slots = features.reshape(tok_rows, -1, BLOCK_SIDE)[:, row_ids, :]
    pre_slot = jnp.einsum(
        "tkc,kch->tkh", x_slots, input_weight_blocks, preferred_element_type=jnp.float32
    )
    pre_act = pre_slot.reshape(tok_rows, groups, BLOCKS_PER_COLUMN, BLOCK_SIDE).sum(2)
    activation, gelu_slope = gelu_pair(pre_act)
    activation = activation.astype(jnp.bfloat16)
    gradient = lax.all_gather(masked, "blk", axis=1, tiled=True)
    gradient_slots = gradient.reshape(tok_rows, -1, BLOCK_SIDE)[:, row_ids, :]
    g_four = gradient_slots.reshape(tok_rows, groups, BLOCKS_PER_COLUMN, BLOCK_SIDE)
    output_share = jnp.einsum(
        "tgh,tgrf->grhf", activation, g_four, preferred_element_type=jnp.float32
    )
    output_share = output_share.reshape(-1, BLOCK_SIDE, BLOCK_SIDE)
    slot_gradient = jnp.einsum(
        "xcn,cpn->xcp", gradient_slots, output_weight_blocks, preferred_element_type=jnp.float32
    )
    grad_act = slot_gradient.reshape(tok_rows, groups, BLOCKS_PER_COLUMN, BLOCK_SIDE).sum(2)
    grad_pre = (grad_act * gelu_slope).astype(jnp.bfloat16)
    x_four = x_slots.reshape(tok_rows, groups, BLOCKS_PER_COLUMN, BLOCK_SIDE)
    input_share = jnp.einsum("tgrc,tgh->grch", x_four, grad_pre, preferred_element_type=jnp.float32)
    input_share = input_share.reshape(-1, BLOCK_SIDE, BLOCK_SIDE)
    in_total, out_total = (
        lax.psum_scatter(
            input_share.astype(jnp.bfloat16), "seq", scatter_dimension=1, tiled=True
        ).astype(jnp.float32),
        lax.psum_scatter(
            output_share.astype(jnp.bfloat16), "seq", scatter_dimension=1, tiled=True
        ).astype(jnp.float32),
    )
    return (in_total.astype(jnp.bfloat16), out_total.astype(jnp.bfloat16))


PLAN_MESH = (8, 4)
NZ = 4
ACROSS = 3
DELIVERY_PARTS = 4
MESH = pl.DeviceIdType.MESH


def pack_gather_grad_kernel(
    tokens_ref, grad_ref, w_in_ref, w_out_ref, ids_ref, len_ref, out_in_ref, out_out_ref,
    chip, lens, give, got, feat, w_in, w_out, part, from_core, to_x, from_x,
    load_sem, core_send, core_recv, x_send, x_recv, z_send, z_recv, y_send, y_recv,
    sum_core_send, sum_core_recv, sum_x_send, sum_x_recv,
):
    rows = chip.shape[2]
    width = chip.shape[3]
    keep = feat.shape[1]
    spare = got.shape[1]
    per = width // BLOCK_SIDE
    n_rows = feat.shape[0] // 2
    groups = part.shape[0]
    pieces = 2 * per
    early = rows - 2 * spare

    blk = lax.axis_index("blk")
    seq = lax.axis_index("seq")
    z, y = blk // 2, blk % 2
    x, core = seq // 2, seq % 2
    core_dev = {"seq": seq + 1 - 2 * core}
    x_dev = {"seq": seq + 2 - 4 * x}
    y_dev = {"blk": blk + 1 - 2 * y}
    up_dev = {"blk": blk + 2}
    down_dev = {"blk": blk - 2}

    def remote(src, dst, send, recv, device):
        return pltpu.make_async_remote_copy(
            src_ref=src, dst_ref=dst, send_sem=send, recv_sem=recv,
            device_id=device, device_id_type=MESH,
        )

    barrier = pltpu.get_barrier_semaphore()
    for device in (core_dev, x_dev, y_dev):
        pl.semaphore_signal(barrier, inc=1, device_id=device, device_id_type=MESH)

    @pl.when(z > 0)
    def _():
        pl.semaphore_signal(barrier, inc=1, device_id=down_dev, device_id_type=MESH)

    @pl.when(z < NZ - 1)
    def _():
        pl.semaphore_signal(barrier, inc=1, device_id=up_dev, device_id_type=MESH)

    own_loads = [
        pltpu.make_async_copy(ref, chip.at[a, core], load_sem.at[a])
        for a, ref in enumerate((tokens_ref, grad_ref))
    ]
    weight_loads = [
        pltpu.make_async_copy(w_in_ref, w_in, load_sem.at[2]),
        pltpu.make_async_copy(w_out_ref, w_out, load_sem.at[3]),
    ]
    for load in own_loads:
        load.start()
    lens[core] = jnp.full(lens.shape[1:], len_ref[0], jnp.int32)
    pl.semaphore_wait(barrier, 3 + jnp.where(z > 0, 1, 0) + jnp.where(z < NZ - 1, 1, 0))

    len_swap = remote(lens.at[core], lens.at[core], core_send.at[2], core_recv.at[2], core_dev)
    len_swap.start()
    swaps = [
        remote(ref, chip.at[a, core], core_send.at[a], core_recv.at[a], core_dev)
        for a, ref in enumerate((tokens_ref, grad_ref))
    ]
    for swap in swaps:
        swap.start()
    len_swap.wait()
    len_a = lens[0][0:1, 0:1]
    len_b = lens[1][0:1, 0:1]
    count = len_a + len_b
    row = lax.broadcasted_iota(jnp.int32, (1, 2 * rows), 1)
    place = jnp.where(
        row < rows,
        jnp.where(row < len_a, row, -1),
        jnp.where(row - rows < len_b, row - rows + len_a, -1),
    )
    odd_give = jnp.bitwise_and(4 * keep - count + core, 1)
    odd_got = jnp.bitwise_and(count + core, 1)
    keep_at = 2 * lax.broadcasted_iota(jnp.int32, (keep, 1), 0) + core
    give_at = 2 * keep + odd_give + 2 * lax.broadcasted_iota(jnp.int32, (spare, 1), 0)
    got_at = count + odd_got + 2 * lax.broadcasted_iota(jnp.int32, (1, spare), 1)
    one, zero = jnp.float32(1), jnp.float32(0)
    pick_early = jnp.where(place == keep_at[:early], one, zero).astype(jnp.bfloat16)
    pick_late = jnp.where(place == keep_at[early:], one, zero).astype(jnp.bfloat16)
    pick_give = jnp.where(place == give_at, one, zero).astype(jnp.bfloat16)
    pick_got = jnp.where(got_at == keep_at[early:], one, zero).astype(jnp.bfloat16)

    def feat_piece(source, late, p):
        at = feat.at[(p // per) * n_rows + per * source + p % per]
        return at.at[pl.ds(early, keep - early)] if late else at.at[pl.ds(0, early)]

    def z_copy(up, source_z, other, late, p, recv_only=False):
        ref = feat_piece(2 * source_z + (1 - y if other else y), late, p)
        slot = p + (2 * pieces if other else pieces if late else 0)
        return remote(
            ref, ref, z_send.at[0 if up else 1, source_z, slot], z_recv.at[source_z, slot],
            y_dev if recv_only else (up_dev if up else down_dev),
        )

    def y_copy(source_z, source_y, late, p):
        ref = feat_piece(2 * source_z + source_y, late, p)
        slot = p + (pieces if late else 0)
        return remote(ref, ref, y_send.at[source_z, slot], y_recv.at[source_z, slot], y_dev)

    def z_both(other, late, p):
        @pl.when(z < NZ - 1)
        def _():
            z_copy(True, z, other, late, p).start()

        @pl.when(z > 0)
        def _():
            z_copy(False, z, other, late, p).start()

    def send_own(late, a):
        def body(i, carry):
            p = a * per + i
            z_both(False, late, p)
            y_copy(z, y, late, p).start()
            return carry

        lax.fori_loop(0, per, body, 0)

    def pass_on(step, late):
        below = z - 1 - step
        above = z + 1 + step

        def arrivals(other, across):
            def body(p, carry):
                @pl.when(below >= 0)
                def _():
                    z_copy(True, below, other, late, p, recv_only=True).wait_recv()

                    @pl.when(z < NZ - 1)
                    def _():
                        z_copy(True, below, other, late, p).start()

                    if not across:
                        y_copy(below, y, late, p).start()

                @pl.when(above < NZ)
                def _():
                    z_copy(False, above, other, late, p, recv_only=True).wait_recv()

                    @pl.when(z > 0)
                    def _():
                        z_copy(False, above, other, late, p).start()

                    if not across:
                        y_copy(above, y, late, p).start()

                return carry

            return body

        if late:
            lax.fori_loop(0, pieces, arrivals(False, False), 0)
        else:
            lax.fori_loop(0, ACROSS, arrivals(False, True), 0)
            lax.fori_loop(ACROSS, pieces, arrivals(False, False), 0)
            lax.fori_loop(0, ACROSS, arrivals(True, True), 0)

    def both(a):
        return chip[a].reshape(2 * rows, width)

    def place_block(block, first, a):
        block = block.astype(jnp.bfloat16)
        for i in range(per):
            feat[a * n_rows + per * blk + i, first : first + block.shape[0]] = block[
                :, i * BLOCK_SIDE : (i + 1) * BLOCK_SIDE
            ]

    for a in range(2):
        own_loads[a].wait()
        swaps[a].wait()
        place_block(jnp.dot(pick_early, both(a), preferred_element_type=jnp.float32), 0, a)
        send_own(False, a)
    for load in weight_loads:
        load.start()
    x_moves = []
    for a in range(2):
        give[a] = jnp.dot(pick_give, both(a), preferred_element_type=jnp.float32).astype(jnp.bfloat16)
        move = remote(give.at[a], got.at[a], x_send.at[a], x_recv.at[a], x_dev)
        move.start()
        x_moves.append(move)

    def turn(p, carry):
        y_copy(z, 1 - y, False, p).wait_recv()
        z_both(True, False, p)
        return carry

    lax.fori_loop(0, ACROSS, turn, 0)
    pass_on(0, False)
    for a in range(2):
        kept = jnp.dot(pick_late, both(a), preferred_element_type=jnp.float32)
        x_moves[a].wait()
        place_block(kept + jnp.dot(pick_got, got[a], preferred_element_type=jnp.float32), early, a)
        send_own(True, a)
    pass_on(1, False)
    pass_on(0, True)
    pass_on(2, False)
    pass_on(1, True)
    pass_on(2, True)

    def end_early(p, carry):
        for source_z in range(NZ):
            y_copy(source_z, 1 - y, False, p).wait_recv()
        return carry

    def end_late(p, carry):
        for source_z in range(NZ):
            y_copy(source_z, 1 - y, True, p).wait_recv()
        return carry

    lax.fori_loop(ACROSS, pieces, end_early, 0)
    lax.fori_loop(0, pieces, end_late, 0)

    for load in weight_loads:
        load.wait()

    def core_sum(g):
        return remote(part.at[g, 1 - core], from_core.at[g], sum_core_send.at[g], sum_core_recv.at[g], core_dev)

    def x_sum(g):
        return remote(to_x.at[g], from_x.at[g], sum_x_send.at[g], sum_x_recv.at[g], x_dev)

    def send_sum(g):
        core_sum(g).wait_recv()
        total = part[g, core, 1 - x].astype(jnp.float32) + from_core[g, 1 - x].astype(jnp.float32)
        to_x[g] = total.astype(jnp.bfloat16)
        x_sum(g).start()

    quarter = BLOCK_SIDE // 4

    def group(g, carry):
        ids = [ids_ref[BLOCKS_PER_COLUMN * g + i] for i in range(BLOCKS_PER_COLUMN)]
        x_cat = jnp.concatenate([feat[r] for r in ids], axis=1)
        g_cat = jnp.concatenate([feat[n_rows + r] for r in ids], axis=1)
        slots = pl.ds(BLOCKS_PER_COLUMN * g, BLOCKS_PER_COLUMN)
        w_rows = w_in[slots].reshape(BLOCKS_PER_COLUMN * BLOCK_SIDE, BLOCK_SIDE)
        wo = w_out[slots]
        w_cols = jnp.concatenate([wo[i] for i in range(BLOCKS_PER_COLUMN)], axis=1)
        pre_act = jnp.dot(x_cat, w_rows, preferred_element_type=jnp.float32)
        grad_act = lax.dot_general(
            g_cat, w_cols, (((1,), (1,)), ((), ())), preferred_element_type=jnp.float32
        )
        activation, gelu_slope = gelu_pair(pre_act)
        activation = activation.astype(jnp.bfloat16)
        grad_pre = (grad_act * gelu_slope).astype(jnp.bfloat16)
        first = (((0,), (0,)), ((), ()))
        share_in = lax.dot_general(grad_pre, x_cat, first, preferred_element_type=jnp.float32)
        share_out = lax.dot_general(activation, g_cat, first, preferred_element_type=jnp.float32)
        for i in range(BLOCKS_PER_COLUMN):
            cols = slice(i * BLOCK_SIDE, (i + 1) * BLOCK_SIDE)
            two = (share_in[:, cols].T, share_out[:, cols])
            for a in range(2):
                rounded = two[a].astype(jnp.bfloat16)
                for q in range(4):
                    part[g, q % 2, q // 2, a, i] = rounded[q * quarter : (q + 1) * quarter]
        core_sum(g).start()

        @pl.when(g > 0)
        def _():
            send_sum(g - 1)

        return carry

    lax.fori_loop(0, groups, group, 0)
    send_sum(groups - 1)

    def finish(g, carry):
        x_sum(g).wait_recv()
        total = (
            part[g, core, x].astype(jnp.float32)
            + from_core[g, x].astype(jnp.float32)
            + from_x[g].astype(jnp.float32)
        ).astype(jnp.bfloat16)
        slots = pl.ds(BLOCKS_PER_COLUMN * g, BLOCKS_PER_COLUMN)
        out_in_ref[slots] = total[0]
        out_out_ref[slots] = total[1]
        return carry

    lax.fori_loop(0, groups, finish, 0)

    def end_sums(g, carry):
        core_sum(g).wait_send()
        x_sum(g).wait_send()
        return carry

    lax.fori_loop(0, groups, end_sums, 0)

    def end_sends(other, late, across):
        def body(p, carry):
            for source_z in range(NZ):
                if across:
                    if not other:
                        @pl.when(source_z == z)
                        def _():
                            y_copy(source_z, y, late, p).wait_send()
                else:
                    y_copy(source_z, y, late, p).wait_send()

                @pl.when(jnp.logical_and(z < NZ - 1, source_z <= z))
                def _():
                    z_copy(True, source_z, other, late, p).wait_send()

                @pl.when(jnp.logical_and(z > 0, source_z >= z))
                def _():
                    z_copy(False, source_z, other, late, p).wait_send()

            return carry

        return body

    lax.fori_loop(0, ACROSS, end_sends(False, False, True), 0)
    lax.fori_loop(ACROSS, pieces, end_sends(False, False, False), 0)
    lax.fori_loop(0, ACROSS, end_sends(True, False, True), 0)
    lax.fori_loop(0, pieces, end_sends(False, True, False), 0)


def deliver_kernel(in_ref, out_ref, in_final, out_final, sems):
    copies = []
    for a, (source, target) in enumerate(((in_ref, in_final), (out_ref, out_final))):
        step = source.shape[0] // DELIVERY_PARTS
        for part in range(DELIVERY_PARTS):
            at = pl.ds(part * step, step)
            copies.append(pltpu.make_async_copy(source.at[at], target.at[at], sems.at[a, part]))
    for copy in copies:
        copy.start()
    for copy in copies:
        copy.wait()


def packed_shards(tokens, grad_out, input_weight_blocks, output_weight_blocks, row_ids, lengths):
    rows, width = tokens.shape
    slots = input_weight_blocks.shape[0]
    groups = slots // BLOCKS_PER_COLUMN
    n_blk, n_seq = PLAN_MESH
    keep = rows * 5 // 8
    spare = rows - keep
    n_rows = n_blk * width // BLOCK_SIDE
    pieces = 2 * width // BLOCK_SIDE
    quarter = BLOCK_SIDE // n_seq
    sums = (2, BLOCKS_PER_COLUMN, quarter, BLOCK_SIDE)
    bf16 = jnp.bfloat16
    dma = pltpu.SemaphoreType.DMA
    any_spec = pl.BlockSpec(memory_space=pl.ANY)
    smem = pl.BlockSpec(memory_space=pltpu.SMEM)
    vmem = pl.BlockSpec(memory_space=pltpu.VMEM)
    out = jax.ShapeDtypeStruct((slots, quarter, BLOCK_SIDE), bf16)
    parts = pl.pallas_call(
        pack_gather_grad_kernel,
        out_shape=(out, out),
        in_specs=[any_spec] * 4 + [smem] * 2,
        out_specs=(vmem, vmem),
        scratch_shapes=[
            pltpu.VMEM((2, 2, rows, width), bf16),
            pltpu.VMEM((2, 8, 128), jnp.int32),
            pltpu.VMEM((2, spare, width), bf16),
            pltpu.VMEM((2, spare, width), bf16),
            pltpu.VMEM((2 * n_rows, keep, BLOCK_SIDE), bf16),
            pltpu.VMEM((slots, BLOCK_SIDE, BLOCK_SIDE), bf16),
            pltpu.VMEM((slots, BLOCK_SIDE, BLOCK_SIDE), bf16),
            pltpu.VMEM((groups, 2, 2) + sums, bf16),
            pltpu.VMEM((groups, 2) + sums, bf16),
            pltpu.VMEM((groups,) + sums, bf16),
            pltpu.VMEM((groups,) + sums, bf16),
            dma((4,)),
            dma((3,)),
            dma((3,)),
            dma((2,)),
            dma((2,)),
            dma((2, NZ, 2 * pieces + ACROSS)),
            dma((NZ, 2 * pieces + ACROSS)),
            dma((NZ, 2 * pieces)),
            dma((NZ, 2 * pieces)),
            dma((groups,)),
            dma((groups,)),
            dma((groups,)),
            dma((groups,)),
        ],
        compiler_params=pltpu.CompilerParams(
            collective_id=0, has_side_effects=True, vmem_limit_bytes=56 * 1024 * 1024
        ),
    )(tokens, grad_out, input_weight_blocks, output_weight_blocks, row_ids, lengths)
    return pl.pallas_call(
        deliver_kernel,
        out_shape=(out, out),
        in_specs=[any_spec] * 2,
        out_specs=(any_spec, any_spec),
        scratch_shapes=[dma((2, DELIVERY_PARTS))],
        compiler_params=pltpu.CompilerParams(vmem_limit_bytes=60 * 1024 * 1024),
    )(*parts)


def solution(mesh):
    return jax.shard_map(
        packed_shards if tuple(mesh.shape.values()) == PLAN_MESH else shards,
        mesh=mesh,
        in_specs=(
            P("seq", "blk"),
            P("seq", "blk"),
            P("blk", None, None),
            P("blk", None, None),
            P("blk"),
            P("seq"),
        ),
        out_specs=(P("blk", "seq", None), P("blk", "seq", None)),
        check_vma=False,
    )
```

```python
import jax
import jax.numpy as jnp
from jax import lax
from jax.experimental import pallas as pl
from jax.experimental.pallas import tpu as pltpu
from jax.sharding import PartitionSpec as P

BLOCK_SIDE = 128
BLOCKS_PER_COLUMN = 4


gelu_scale = 0.7978845608


def gelu_pair(pre_act):
    tanh_val = jnp.tanh(gelu_scale * (pre_act + 0.044715 * pre_act * pre_act * pre_act))
    activation = 0.5 * pre_act * (1.0 + tanh_val)
    gelu_slope = 0.5 * (1.0 + tanh_val) + 0.5 * pre_act * (
        1.0 - tanh_val * tanh_val
    ) * gelu_scale * (1.0 + 0.134145 * pre_act * pre_act)
    return (activation, gelu_slope)


def shards(tokens, grad_out, input_weight_blocks, output_weight_blocks, row_ids, lengths):
    tok_rows = tokens.shape[0]
    groups = input_weight_blocks.shape[0] // BLOCKS_PER_COLUMN
    live_rows = lax.iota(jnp.int32, tok_rows)[:, None] < lengths[0]
    masked = jnp.where(live_rows, grad_out, jnp.zeros_like(grad_out))
    features = lax.all_gather(tokens, "blk", axis=1, tiled=True)
    x_slots = features.reshape(tok_rows, -1, BLOCK_SIDE)[:, row_ids, :]
    pre_slot = jnp.einsum(
        "tkc,kch->tkh", x_slots, input_weight_blocks, preferred_element_type=jnp.float32
    )
    pre_act = pre_slot.reshape(tok_rows, groups, BLOCKS_PER_COLUMN, BLOCK_SIDE).sum(2)
    activation, gelu_slope = gelu_pair(pre_act)
    activation = activation.astype(jnp.bfloat16)
    gradient = lax.all_gather(masked, "blk", axis=1, tiled=True)
    gradient_slots = gradient.reshape(tok_rows, -1, BLOCK_SIDE)[:, row_ids, :]
    g_four = gradient_slots.reshape(tok_rows, groups, BLOCKS_PER_COLUMN, BLOCK_SIDE)
    output_share = jnp.einsum(
        "tgh,tgrf->grhf", activation, g_four, preferred_element_type=jnp.float32
    )
    output_share = output_share.reshape(-1, BLOCK_SIDE, BLOCK_SIDE)
    slot_gradient = jnp.einsum(
        "xcn,cpn->xcp", gradient_slots, output_weight_blocks, preferred_element_type=jnp.float32
    )
    grad_act = slot_gradient.reshape(tok_rows, groups, BLOCKS_PER_COLUMN, BLOCK_SIDE).sum(2)
    grad_pre = (grad_act * gelu_slope).astype(jnp.bfloat16)
    x_four = x_slots.reshape(tok_rows, groups, BLOCKS_PER_COLUMN, BLOCK_SIDE)
    input_share = jnp.einsum("tgrc,tgh->grch", x_four, grad_pre, preferred_element_type=jnp.float32)
    input_share = input_share.reshape(-1, BLOCK_SIDE, BLOCK_SIDE)
    in_total, out_total = (
        lax.psum_scatter(
            input_share.astype(jnp.bfloat16), "seq", scatter_dimension=1, tiled=True
        ).astype(jnp.float32),
        lax.psum_scatter(
            output_share.astype(jnp.bfloat16), "seq", scatter_dimension=1, tiled=True
        ).astype(jnp.float32),
    )
    return (in_total.astype(jnp.bfloat16), out_total.astype(jnp.bfloat16))


PLAN_MESH = (8, 4)
NZ = 4
ACROSS = 3
TOGETHER = 2
DELIVERY_PARTS = 4
MESH = pl.DeviceIdType.MESH


def pack_gather_grad_kernel(
    tokens_ref, grad_ref, w_in_ref, w_out_ref, ids_ref, len_ref, out_in_ref, out_out_ref,
    chip, lens, give, got, feat, w_in, w_out, part, from_core, to_x, from_x, staged,
    load_sem, core_send, core_recv, x_send, x_recv, z_send, z_recv, y_send, y_recv,
    sum_core_send, sum_core_recv, sum_x_send, sum_x_recv, store_sem,
):
    rows = chip.shape[2]
    width = chip.shape[3]
    keep = feat.shape[1]
    spare = got.shape[1]
    per = width // BLOCK_SIDE
    n_rows = feat.shape[0] // 2
    groups = part.shape[1]
    pieces = 2 * per
    early = rows - 2 * spare

    blk = lax.axis_index("blk")
    seq = lax.axis_index("seq")
    z, y = blk // 2, blk % 2
    x, core = seq // 2, seq % 2
    core_dev = {"seq": seq + 1 - 2 * core}
    x_dev = {"seq": seq + 2 - 4 * x}
    y_dev = {"blk": blk + 1 - 2 * y}
    up_dev = {"blk": blk + 2}
    down_dev = {"blk": blk - 2}

    def remote(src, dst, send, recv, device):
        return pltpu.make_async_remote_copy(
            src_ref=src, dst_ref=dst, send_sem=send, recv_sem=recv,
            device_id=device, device_id_type=MESH,
        )

    barrier = pltpu.get_barrier_semaphore()
    for device in (core_dev, x_dev, y_dev):
        pl.semaphore_signal(barrier, inc=1, device_id=device, device_id_type=MESH)

    @pl.when(z > 0)
    def _():
        pl.semaphore_signal(barrier, inc=1, device_id=down_dev, device_id_type=MESH)

    @pl.when(z < NZ - 1)
    def _():
        pl.semaphore_signal(barrier, inc=1, device_id=up_dev, device_id_type=MESH)

    own_loads = [
        pltpu.make_async_copy(ref, chip.at[a, core], load_sem.at[a])
        for a, ref in enumerate((tokens_ref, grad_ref))
    ]
    weight_loads = [
        pltpu.make_async_copy(w_in_ref, w_in, load_sem.at[2]),
        pltpu.make_async_copy(w_out_ref, w_out, load_sem.at[3]),
    ]
    for load in own_loads:
        load.start()
    lens[core] = jnp.full(lens.shape[1:], len_ref[0], jnp.int32)
    pl.semaphore_wait(barrier, 3 + jnp.where(z > 0, 1, 0) + jnp.where(z < NZ - 1, 1, 0))

    len_swap = remote(lens.at[core], lens.at[core], core_send.at[2], core_recv.at[2], core_dev)
    len_swap.start()
    swaps = [
        remote(ref, chip.at[a, core], core_send.at[a], core_recv.at[a], core_dev)
        for a, ref in enumerate((tokens_ref, grad_ref))
    ]
    for swap in swaps:
        swap.start()
    len_swap.wait()
    len_a = lens[0][0:1, 0:1]
    len_b = lens[1][0:1, 0:1]
    count = len_a + len_b
    row = lax.broadcasted_iota(jnp.int32, (1, 2 * rows), 1)
    place = jnp.where(
        row < rows,
        jnp.where(row < len_a, row, -1),
        jnp.where(row - rows < len_b, row - rows + len_a, -1),
    )
    odd_give = jnp.bitwise_and(4 * keep - count + core, 1)
    odd_got = jnp.bitwise_and(count + core, 1)
    keep_at = 2 * lax.broadcasted_iota(jnp.int32, (keep, 1), 0) + core
    give_at = 2 * keep + odd_give + 2 * lax.broadcasted_iota(jnp.int32, (spare, 1), 0)
    got_at = count + odd_got + 2 * lax.broadcasted_iota(jnp.int32, (1, spare), 1)
    one, zero = jnp.float32(1), jnp.float32(0)
    pick_early = jnp.where(place == keep_at[:early], one, zero).astype(jnp.bfloat16)
    pick_late = jnp.where(place == keep_at[early:], one, zero).astype(jnp.bfloat16)
    pick_give = jnp.where(place == give_at, one, zero).astype(jnp.bfloat16)
    pick_got = jnp.where(got_at == keep_at[early:], one, zero).astype(jnp.bfloat16)

    def feat_piece(source, late, p):
        at = feat.at[(p // per) * n_rows + per * source + p % per]
        return at.at[pl.ds(early, keep - early)] if late else at.at[pl.ds(0, early)]

    def z_copy(up, source_z, other, late, p, recv_only=False):
        ref = feat_piece(2 * source_z + (1 - y if other else y), late, p)
        slot = p + (2 * pieces if other else pieces if late else 0)
        return remote(
            ref, ref, z_send.at[0 if up else 1, source_z, slot], z_recv.at[source_z, slot],
            y_dev if recv_only else (up_dev if up else down_dev),
        )

    def y_copy(source_z, source_y, late, p):
        ref = feat_piece(2 * source_z + source_y, late, p)
        slot = p + (pieces if late else 0)
        return remote(ref, ref, y_send.at[source_z, slot], y_recv.at[source_z, slot], y_dev)

    def z_both(other, late, p):
        @pl.when(z < NZ - 1)
        def _():
            z_copy(True, z, other, late, p).start()

        @pl.when(z > 0)
        def _():
            z_copy(False, z, other, late, p).start()

    def send_own(late, a):
        def body(i, carry):
            p = a * per + i
            z_both(False, late, p)
            y_copy(z, y, late, p).start()
            return carry

        lax.fori_loop(0, per, body, 0)

    def pass_on(step, late):
        below = z - 1 - step
        above = z + 1 + step

        def arrivals(other, across):
            def body(p, carry):
                @pl.when(below >= 0)
                def _():
                    z_copy(True, below, other, late, p, recv_only=True).wait_recv()

                    @pl.when(z < NZ - 1)
                    def _():
                        z_copy(True, below, other, late, p).start()

                    if not across:
                        y_copy(below, y, late, p).start()

                @pl.when(above < NZ)
                def _():
                    z_copy(False, above, other, late, p, recv_only=True).wait_recv()

                    @pl.when(z > 0)
                    def _():
                        z_copy(False, above, other, late, p).start()

                    if not across:
                        y_copy(above, y, late, p).start()

                return carry

            return body

        if late:
            lax.fori_loop(0, pieces, arrivals(False, False), 0)
        else:
            lax.fori_loop(0, ACROSS, arrivals(False, True), 0)
            lax.fori_loop(ACROSS, pieces, arrivals(False, False), 0)
            lax.fori_loop(0, ACROSS, arrivals(True, True), 0)

    def both(a):
        return chip[a].reshape(2 * rows, width)

    def place_block(block, first, a):
        block = block.astype(jnp.bfloat16)
        for i in range(per):
            feat[a * n_rows + per * blk + i, first : first + block.shape[0]] = block[
                :, i * BLOCK_SIDE : (i + 1) * BLOCK_SIDE
            ]

    for a in range(2):
        own_loads[a].wait()
        swaps[a].wait()
        place_block(jnp.dot(pick_early, both(a), preferred_element_type=jnp.float32), 0, a)
        send_own(False, a)
    for load in weight_loads:
        load.start()
    x_moves = []
    for a in range(2):
        give[a] = jnp.dot(pick_give, both(a), preferred_element_type=jnp.float32).astype(jnp.bfloat16)
        move = remote(give.at[a], got.at[a], x_send.at[a], x_recv.at[a], x_dev)
        move.start()
        x_moves.append(move)

    def turn(p, carry):
        y_copy(z, 1 - y, False, p).wait_recv()
        z_both(True, False, p)
        return carry

    lax.fori_loop(0, ACROSS, turn, 0)
    pass_on(0, False)
    for a in range(2):
        kept = jnp.dot(pick_late, both(a), preferred_element_type=jnp.float32)
        x_moves[a].wait()
        place_block(kept + jnp.dot(pick_got, got[a], preferred_element_type=jnp.float32), early, a)
        send_own(True, a)
    pass_on(1, False)
    pass_on(0, True)
    pass_on(2, False)
    pass_on(1, True)
    pass_on(2, True)

    def end_early(p, carry):
        for source_z in range(NZ):
            y_copy(source_z, 1 - y, False, p).wait_recv()
        return carry

    def end_late(p, carry):
        for source_z in range(NZ):
            y_copy(source_z, 1 - y, True, p).wait_recv()
        return carry

    lax.fori_loop(ACROSS, pieces, end_early, 0)
    lax.fori_loop(0, pieces, end_late, 0)

    for load in weight_loads:
        load.wait()

    turns = groups // TOGETHER

    def span(t):
        return pl.ds(TOGETHER * t, TOGETHER)

    def core_sum(t):
        return remote(
            part.at[1 - core, span(t)], from_core.at[span(t)],
            sum_core_send.at[t], sum_core_recv.at[t], core_dev,
        )

    def x_sum(t):
        return remote(
            to_x.at[span(t)], from_x.at[span(t)], sum_x_send.at[t], sum_x_recv.at[t], x_dev
        )

    def send_sum(t):
        core_sum(t).wait_recv()
        total = part[core, span(t), 1 - x].astype(jnp.float32)
        total = total + from_core[span(t), 1 - x].astype(jnp.float32)
        to_x[span(t)] = total.astype(jnp.bfloat16)
        x_sum(t).start()

    quarter = BLOCK_SIDE // 4
    first = (((0,), (0,)), ((), ()))

    def column_inputs(g):
        ids = [ids_ref[BLOCKS_PER_COLUMN * g + i] for i in range(BLOCKS_PER_COLUMN)]
        x_cat = jnp.concatenate([feat[r] for r in ids], axis=1)
        g_cat = jnp.concatenate([feat[n_rows + r] for r in ids], axis=1)
        slots = pl.ds(BLOCKS_PER_COLUMN * g, BLOCKS_PER_COLUMN)
        w_rows = w_in[slots].reshape(BLOCKS_PER_COLUMN * BLOCK_SIDE, BLOCK_SIDE)
        wo = w_out[slots]
        w_cols = jnp.concatenate([wo[i] for i in range(BLOCKS_PER_COLUMN)], axis=1)
        pre_act = jnp.dot(x_cat, w_rows, preferred_element_type=jnp.float32)
        grad_act = lax.dot_general(
            g_cat, w_cols, (((1,), (1,)), ((), ())), preferred_element_type=jnp.float32
        )
        return x_cat, g_cat, pre_act, grad_act

    def column_grads(g, x_cat, g_cat, pre_act, grad_act):
        activation, gelu_slope = gelu_pair(pre_act)
        activation = activation.astype(jnp.bfloat16)
        grad_pre = (grad_act * gelu_slope).astype(jnp.bfloat16)
        share_in = lax.dot_general(grad_pre, x_cat, first, preferred_element_type=jnp.float32)
        share_out = lax.dot_general(activation, g_cat, first, preferred_element_type=jnp.float32)
        share_in = share_in.astype(jnp.bfloat16)
        share_out = share_out.astype(jnp.bfloat16)
        for i in range(BLOCKS_PER_COLUMN):
            cols = slice(i * BLOCK_SIDE, (i + 1) * BLOCK_SIDE)
            two = (share_in[:, cols].T, share_out[:, cols])
            for a in range(2):
                for q in range(4):
                    part[q % 2, g, q // 2, a, i] = two[a][q * quarter : (q + 1) * quarter]

    def turn_columns(t, carry):
        columns = [TOGETHER * t + u for u in range(TOGETHER)]
        held = [column_inputs(g) for g in columns]
        for g, values in zip(columns, held):
            column_grads(g, *values)
        core_sum(t).start()

        @pl.when(t > 0)
        def _():
            send_sum(t - 1)

        return carry

    lax.fori_loop(0, turns, turn_columns, 0)
    send_sum(turns - 1)

    per_turn = TOGETHER * BLOCKS_PER_COLUMN

    def stores(t):
        at = pl.ds(per_turn * t, per_turn)
        return [
            pltpu.make_async_copy(staged.at[a, at], ref.at[at], store_sem.at[a, t])
            for a, ref in enumerate((out_in_ref, out_out_ref))
        ]

    def finish(t, carry):
        x_sum(t).wait_recv()
        total = (
            part[core, span(t), x].astype(jnp.float32)
            + from_core[span(t), x].astype(jnp.float32)
            + from_x[span(t)].astype(jnp.float32)
        ).astype(jnp.bfloat16)
        for u in range(TOGETHER):
            at = pl.ds(per_turn * t + u * BLOCKS_PER_COLUMN, BLOCKS_PER_COLUMN)
            for a in range(2):
                staged[a, at] = total[u, a]
        for store in stores(t):
            store.start()
        return carry

    lax.fori_loop(0, turns, finish, 0)

    def end_sums(t, carry):
        core_sum(t).wait_send()
        x_sum(t).wait_send()
        for store in stores(t):
            store.wait()
        return carry

    lax.fori_loop(0, turns, end_sums, 0)

    def end_sends(other, late, across):
        def body(p, carry):
            for source_z in range(NZ):
                if across:
                    if not other:
                        @pl.when(source_z == z)
                        def _():
                            y_copy(source_z, y, late, p).wait_send()
                else:
                    y_copy(source_z, y, late, p).wait_send()

                @pl.when(jnp.logical_and(z < NZ - 1, source_z <= z))
                def _():
                    z_copy(True, source_z, other, late, p).wait_send()

                @pl.when(jnp.logical_and(z > 0, source_z >= z))
                def _():
                    z_copy(False, source_z, other, late, p).wait_send()

            return carry

        return body

    lax.fori_loop(0, ACROSS, end_sends(False, False, True), 0)
    lax.fori_loop(ACROSS, pieces, end_sends(False, False, False), 0)
    lax.fori_loop(0, ACROSS, end_sends(True, False, True), 0)
    lax.fori_loop(0, pieces, end_sends(False, True, False), 0)


def deliver_kernel(in_ref, out_ref, in_final, out_final, held, sems):
    pairs = []
    for a, (source, target) in enumerate(((in_ref, in_final), (out_ref, out_final))):
        step = source.shape[0] // DELIVERY_PARTS
        for k in range(DELIVERY_PARTS):
            at = pl.ds(k * step, step)
            pairs.append((
                pltpu.make_async_copy(source.at[at], held.at[a, at], sems.at[0, a, k]),
                pltpu.make_async_copy(held.at[a, at], target.at[at], sems.at[1, a, k]),
            ))
    for load, store in pairs:
        load.start()
    for load, store in pairs:
        load.wait()
        store.start()
    for load, store in pairs:
        store.wait()


def packed_shards(tokens, grad_out, input_weight_blocks, output_weight_blocks, row_ids, lengths):
    rows, width = tokens.shape
    slots = input_weight_blocks.shape[0]
    groups = slots // BLOCKS_PER_COLUMN
    n_blk, n_seq = PLAN_MESH
    keep = rows * 5 // 8
    spare = rows - keep
    n_rows = n_blk * width // BLOCK_SIDE
    pieces = 2 * width // BLOCK_SIDE
    quarter = BLOCK_SIDE // n_seq
    sums = (2, BLOCKS_PER_COLUMN, quarter, BLOCK_SIDE)
    bf16 = jnp.bfloat16
    dma = pltpu.SemaphoreType.DMA
    any_spec = pl.BlockSpec(memory_space=pl.ANY)
    smem = pl.BlockSpec(memory_space=pltpu.SMEM)
    out = jax.ShapeDtypeStruct((slots, quarter, BLOCK_SIDE), bf16)
    parts = pl.pallas_call(
        pack_gather_grad_kernel,
        out_shape=(out, out),
        in_specs=[any_spec] * 4 + [smem] * 2,
        out_specs=(any_spec, any_spec),
        scratch_shapes=[
            pltpu.VMEM((2, 2, rows, width), bf16),
            pltpu.VMEM((2, 8, 128), jnp.int32),
            pltpu.VMEM((2, spare, width), bf16),
            pltpu.VMEM((2, spare, width), bf16),
            pltpu.VMEM((2 * n_rows, keep, BLOCK_SIDE), bf16),
            pltpu.VMEM((slots, BLOCK_SIDE, BLOCK_SIDE), bf16),
            pltpu.VMEM((slots, BLOCK_SIDE, BLOCK_SIDE), bf16),
            pltpu.VMEM((2, groups, 2) + sums, bf16),
            pltpu.VMEM((groups, 2) + sums, bf16),
            pltpu.VMEM((groups,) + sums, bf16),
            pltpu.VMEM((groups,) + sums, bf16),
            pltpu.VMEM((2, slots, quarter, BLOCK_SIDE), bf16),
            dma((4,)),
            dma((3,)),
            dma((3,)),
            dma((2,)),
            dma((2,)),
            dma((2, NZ, 2 * pieces + ACROSS)),
            dma((NZ, 2 * pieces + ACROSS)),
            dma((NZ, 2 * pieces)),
            dma((NZ, 2 * pieces)),
            dma((groups // TOGETHER,)),
            dma((groups // TOGETHER,)),
            dma((groups // TOGETHER,)),
            dma((groups // TOGETHER,)),
            dma((2, groups // TOGETHER)),
        ],
        compiler_params=pltpu.CompilerParams(
            collective_id=0, has_side_effects=True, vmem_limit_bytes=56 * 1024 * 1024
        ),
    )(tokens, grad_out, input_weight_blocks, output_weight_blocks, row_ids, lengths)
    return pl.pallas_call(
        deliver_kernel,
        out_shape=(out, out),
        in_specs=[any_spec] * 2,
        out_specs=(any_spec, any_spec),
        scratch_shapes=[
            pltpu.VMEM((2, slots, quarter, BLOCK_SIDE), bf16),
            dma((2, 2, DELIVERY_PARTS)),
        ],
        compiler_params=pltpu.CompilerParams(vmem_limit_bytes=60 * 1024 * 1024),
    )(*parts)


def solution(mesh):
    return jax.shard_map(
        packed_shards if tuple(mesh.shape.values()) == PLAN_MESH else shards,
        mesh=mesh,
        in_specs=(
            P("seq", "blk"),
            P("seq", "blk"),
            P("blk", None, None),
            P("blk", None, None),
            P("blk"),
            P("seq"),
        ),
        out_specs=(P("blk", "seq", None), P("blk", "seq", None)),
        check_vma=False,
    )
```

```python
import jax
import jax.numpy as jnp
from jax import lax
from jax.experimental import pallas as pl
from jax.experimental.pallas import tpu as pltpu
from jax.sharding import PartitionSpec as P

BLOCK_SIDE = 128
BLOCKS_PER_COLUMN = 4


gelu_scale = 0.7978845608


def gelu_pair(pre_act):
    tanh_val = jnp.tanh(gelu_scale * (pre_act + 0.044715 * pre_act * pre_act * pre_act))
    activation = 0.5 * pre_act * (1.0 + tanh_val)
    gelu_slope = 0.5 * (1.0 + tanh_val) + 0.5 * pre_act * (
        1.0 - tanh_val * tanh_val
    ) * gelu_scale * (1.0 + 0.134145 * pre_act * pre_act)
    return (activation, gelu_slope)


def shards(tokens, grad_out, input_weight_blocks, output_weight_blocks, row_ids, lengths):
    tok_rows = tokens.shape[0]
    groups = input_weight_blocks.shape[0] // BLOCKS_PER_COLUMN
    live_rows = lax.iota(jnp.int32, tok_rows)[:, None] < lengths[0]
    masked = jnp.where(live_rows, grad_out, jnp.zeros_like(grad_out))
    features = lax.all_gather(tokens, "blk", axis=1, tiled=True)
    x_slots = features.reshape(tok_rows, -1, BLOCK_SIDE)[:, row_ids, :]
    pre_slot = jnp.einsum(
        "tkc,kch->tkh", x_slots, input_weight_blocks, preferred_element_type=jnp.float32
    )
    pre_act = pre_slot.reshape(tok_rows, groups, BLOCKS_PER_COLUMN, BLOCK_SIDE).sum(2)
    activation, gelu_slope = gelu_pair(pre_act)
    activation = activation.astype(jnp.bfloat16)
    gradient = lax.all_gather(masked, "blk", axis=1, tiled=True)
    gradient_slots = gradient.reshape(tok_rows, -1, BLOCK_SIDE)[:, row_ids, :]
    g_four = gradient_slots.reshape(tok_rows, groups, BLOCKS_PER_COLUMN, BLOCK_SIDE)
    output_share = jnp.einsum(
        "tgh,tgrf->grhf", activation, g_four, preferred_element_type=jnp.float32
    )
    output_share = output_share.reshape(-1, BLOCK_SIDE, BLOCK_SIDE)
    slot_gradient = jnp.einsum(
        "xcn,cpn->xcp", gradient_slots, output_weight_blocks, preferred_element_type=jnp.float32
    )
    grad_act = slot_gradient.reshape(tok_rows, groups, BLOCKS_PER_COLUMN, BLOCK_SIDE).sum(2)
    grad_pre = (grad_act * gelu_slope).astype(jnp.bfloat16)
    x_four = x_slots.reshape(tok_rows, groups, BLOCKS_PER_COLUMN, BLOCK_SIDE)
    input_share = jnp.einsum("tgrc,tgh->grch", x_four, grad_pre, preferred_element_type=jnp.float32)
    input_share = input_share.reshape(-1, BLOCK_SIDE, BLOCK_SIDE)
    in_total, out_total = (
        lax.psum_scatter(
            input_share.astype(jnp.bfloat16), "seq", scatter_dimension=1, tiled=True
        ).astype(jnp.float32),
        lax.psum_scatter(
            output_share.astype(jnp.bfloat16), "seq", scatter_dimension=1, tiled=True
        ).astype(jnp.float32),
    )
    return (in_total.astype(jnp.bfloat16), out_total.astype(jnp.bfloat16))


PLAN_MESH = (8, 4)
NZ = 4
ACROSS = 3
TOGETHER = 2
DELIVERY_PARTS = 4
MESH = pl.DeviceIdType.MESH


def pack_gather_grad_kernel(
    tokens_ref, grad_ref, w_in_ref, w_out_ref, ids_ref, len_ref, out_in_ref, out_out_ref,
    chip, lens, give, got, feat, w_in, w_out, part, from_core, to_x, from_x, staged,
    feat_shared, part_shared, shared_core,
    load_sem, core_send, core_recv, x_send, x_recv, z_send, z_recv, y_send, y_recv,
    sum_core_send, sum_core_recv, sum_x_send, sum_x_recv, store_sem,
    sz_send, sz_recv, sy_send, sy_recv, sx_send, sx_recv, sc_send, sc_recv,
):
    rows = chip.shape[2]
    width = chip.shape[3]
    solo = feat.shape[1]
    origin = feat_shared.shape[2]
    keep = solo + origin
    spare = got.shape[1]
    per = width // BLOCK_SIDE
    n_rows = feat.shape[0] // 2
    groups = part.shape[1]
    pieces = 2 * per
    early = rows - 2 * spare
    head = 2 * early
    halves = (pl.ds(0, head), pl.ds(head, rows - head))

    blk = lax.axis_index("blk")
    seq = lax.axis_index("seq")
    z, y = blk // 2, blk % 2
    x, core = seq // 2, seq % 2
    core_dev = {"seq": seq + 1 - 2 * core}
    x_dev = {"seq": seq + 2 - 4 * x}
    y_dev = {"blk": blk + 1 - 2 * y}
    up_dev = {"blk": blk + 2}
    down_dev = {"blk": blk - 2}

    def remote(src, dst, send, recv, device):
        return pltpu.make_async_remote_copy(
            src_ref=src, dst_ref=dst, send_sem=send, recv_sem=recv,
            device_id=device, device_id_type=MESH,
        )

    barrier = pltpu.get_barrier_semaphore()
    for device in (core_dev, x_dev, y_dev):
        pl.semaphore_signal(barrier, inc=1, device_id=device, device_id_type=MESH)

    @pl.when(z > 0)
    def _():
        pl.semaphore_signal(barrier, inc=1, device_id=down_dev, device_id_type=MESH)

    @pl.when(z < NZ - 1)
    def _():
        pl.semaphore_signal(barrier, inc=1, device_id=up_dev, device_id_type=MESH)

    own_loads = [
        pltpu.make_async_copy(ref, chip.at[a, core], load_sem.at[a])
        for a, ref in enumerate((tokens_ref, grad_ref))
    ]
    weight_loads = [
        pltpu.make_async_copy(w_in_ref, w_in, load_sem.at[2]),
        pltpu.make_async_copy(w_out_ref, w_out, load_sem.at[3]),
    ]
    for load in own_loads:
        load.start()
    lens[core] = jnp.full(lens.shape[1:], len_ref[0], jnp.int32)
    pl.semaphore_wait(barrier, 3 + jnp.where(z > 0, 1, 0) + jnp.where(z < NZ - 1, 1, 0))

    len_swap = remote(lens.at[core], lens.at[core], core_send.at[4], core_recv.at[4], core_dev)
    len_swap.start()
    swaps = [
        [
            remote(
                ref.at[half], chip.at[a, core, half],
                core_send.at[2 * h + a], core_recv.at[2 * h + a], core_dev,
            )
            for a, ref in enumerate((tokens_ref, grad_ref))
        ]
        for h, half in enumerate(halves)
    ]
    for swap in swaps[0] + swaps[1]:
        swap.start()
    len_swap.wait()
    len_a = lens[0][0:1, 0:1]
    len_b = lens[1][0:1, 0:1]
    count = len_a + len_b

    def places(held):
        row = lax.broadcasted_iota(jnp.int32, (1, 2 * held), 1)
        return jnp.where(
            row < held,
            jnp.where(row < len_a, row, -1),
            jnp.where(row - held < len_b, row - held + len_a, -1),
        )

    place = places(rows)
    odd_give = jnp.bitwise_and(4 * keep - count + core, 1)
    odd_got = jnp.bitwise_and(count + core, 1)
    keep_at = 2 * lax.broadcasted_iota(jnp.int32, (keep, 1), 0) + core
    give_at = 2 * keep + odd_give + 2 * lax.broadcasted_iota(jnp.int32, (spare, 1), 0)
    got_at = count + odd_got + 2 * lax.broadcasted_iota(jnp.int32, (1, spare), 1)
    one, zero = jnp.float32(1), jnp.float32(0)
    pick_early = jnp.where(places(head) == keep_at[:early], one, zero).astype(jnp.bfloat16)
    pick_late = jnp.where(place == keep_at[early:], one, zero).astype(jnp.bfloat16)
    pick_give = jnp.where(place == give_at, one, zero).astype(jnp.bfloat16)
    pick_got = jnp.where(got_at == keep_at[early:], one, zero).astype(jnp.bfloat16)

    def feat_piece(source, late, p):
        at = feat.at[(p // per) * n_rows + per * source + p % per]
        return at.at[pl.ds(early, solo - early)] if late else at.at[pl.ds(0, early)]

    def z_copy(up, source_z, other, late, p, recv_only=False):
        ref = feat_piece(2 * source_z + (1 - y if other else y), late, p)
        slot = p + (2 * pieces if other else pieces if late else 0)
        return remote(
            ref, ref, z_send.at[0 if up else 1, source_z, slot], z_recv.at[source_z, slot],
            y_dev if recv_only else (up_dev if up else down_dev),
        )

    def y_copy(source_z, source_y, late, p):
        ref = feat_piece(2 * source_z + source_y, late, p)
        slot = p + (pieces if late else 0)
        return remote(ref, ref, y_send.at[source_z, slot], y_recv.at[source_z, slot], y_dev)

    def z_both(other, late, p):
        @pl.when(z < NZ - 1)
        def _():
            z_copy(True, z, other, late, p).start()

        @pl.when(z > 0)
        def _():
            z_copy(False, z, other, late, p).start()

    def send_own(late, a):
        def body(i, carry):
            p = a * per + i
            z_both(False, late, p)
            y_copy(z, y, late, p).start()
            return carry

        lax.fori_loop(0, per, body, 0)

    def pass_on(step, late):
        below = z - 1 - step
        above = z + 1 + step

        def arrivals(other, across):
            def body(p, carry):
                @pl.when(below >= 0)
                def _():
                    z_copy(True, below, other, late, p, recv_only=True).wait_recv()

                    @pl.when(z < NZ - 1)
                    def _():
                        z_copy(True, below, other, late, p).start()

                    if not across:
                        y_copy(below, y, late, p).start()

                @pl.when(above < NZ)
                def _():
                    z_copy(False, above, other, late, p, recv_only=True).wait_recv()

                    @pl.when(z > 0)
                    def _():
                        z_copy(False, above, other, late, p).start()

                    if not across:
                        y_copy(above, y, late, p).start()

                return carry

            return body

        if late:
            lax.fori_loop(0, pieces, arrivals(False, False), 0)
        else:
            lax.fori_loop(0, ACROSS, arrivals(False, True), 0)
            lax.fori_loop(ACROSS, pieces, arrivals(False, False), 0)
            lax.fori_loop(0, ACROSS, arrivals(True, True), 0)

    def both(a):
        return chip[a].reshape(2 * rows, width)

    def place_block(block, first, a):
        block = block.astype(jnp.bfloat16)
        for i in range(per):
            feat[a * n_rows + per * blk + i, first : first + block.shape[0]] = block[
                :, i * BLOCK_SIDE : (i + 1) * BLOCK_SIDE
            ]

    def share_x(a):
        ref = feat_shared.at[pl.ds(a * n_rows + per * blk, per), x]
        return remote(ref, ref, sx_send.at[a], sx_recv.at[a], x_dev)

    def shared_piece(source, p):
        return feat_shared.at[(p // per) * n_rows + per * source + p % per]

    def shared_z(up, source_z, p, recv_only=False):
        ref = shared_piece(2 * source_z + y, p)
        return remote(
            ref, ref, sz_send.at[0 if up else 1, source_z, p], sz_recv.at[source_z, p],
            y_dev if recv_only else (up_dev if up else down_dev),
        )

    def shared_y(source_z, source_y, p):
        ref = shared_piece(2 * source_z + source_y, p)
        return remote(ref, ref, sy_send.at[source_z, p], sy_recv.at[source_z, p], y_dev)

    def send_shared(p, carry):
        shared_y(z, y, p).start()

        @pl.when(z < NZ - 1)
        def _():
            shared_z(True, z, p).start()

        @pl.when(z > 0)
        def _():
            shared_z(False, z, p).start()

        return carry

    def pass_shared(k, carry):
        step, p = k // pieces, k % pieces
        below = z - 1 - step
        above = z + 1 + step

        @pl.when(below >= 0)
        def _():
            shared_z(True, below, p, recv_only=True).wait_recv()

            @pl.when(z < NZ - 1)
            def _():
                shared_z(True, below, p).start()

            shared_y(below, y, p).start()

        @pl.when(above < NZ)
        def _():
            shared_z(False, above, p, recv_only=True).wait_recv()

            @pl.when(z > 0)
            def _():
                shared_z(False, above, p).start()

            shared_y(above, y, p).start()

        return carry

    for a in range(2):
        own_loads[a].wait()
        swaps[0][a].wait()
        heads = chip[a, :, :head].reshape(2 * head, width)
        place_block(jnp.dot(pick_early, heads, preferred_element_type=jnp.float32), 0, a)
        send_own(False, a)
    for load in weight_loads:
        load.start()
    x_moves = []
    for a in range(2):
        swaps[1][a].wait()
        give[a] = jnp.dot(pick_give, both(a), preferred_element_type=jnp.float32).astype(jnp.bfloat16)
        move = remote(give.at[a], got.at[a], x_send.at[a], x_recv.at[a], x_dev)
        move.start()
        x_moves.append(move)

    def turn(p, carry):
        y_copy(z, 1 - y, False, p).wait_recv()
        z_both(True, False, p)
        return carry

    lax.fori_loop(0, ACROSS, turn, 0)
    pass_on(0, False)
    for a in range(2):
        kept = jnp.dot(pick_late, both(a), preferred_element_type=jnp.float32)
        x_moves[a].wait()
        kept = kept + jnp.dot(pick_got, got[a], preferred_element_type=jnp.float32)
        place_block(kept[: solo - early], early, a)
        send_own(True, a)
        last = kept[solo - early :].astype(jnp.bfloat16)
        for i in range(per):
            feat_shared[a * n_rows + per * blk + i, x] = last[
                :, i * BLOCK_SIDE : (i + 1) * BLOCK_SIDE
            ]
        share_x(a).start()
    pass_on(1, False)
    pass_on(0, True)
    pass_on(2, False)
    pass_on(1, True)
    pass_on(2, True)
    for a in range(2):
        share_x(a).wait()
    lax.fori_loop(0, pieces, send_shared, 0)

    def end_early(p, carry):
        for source_z in range(NZ):
            y_copy(source_z, 1 - y, False, p).wait_recv()
        return carry

    def end_late(p, carry):
        for source_z in range(NZ):
            y_copy(source_z, 1 - y, True, p).wait_recv()
        return carry

    lax.fori_loop(ACROSS, pieces, end_early, 0)
    lax.fori_loop(0, pieces, end_late, 0)

    for load in weight_loads:
        load.wait()

    turns = groups // TOGETHER

    def span(t):
        return pl.ds(TOGETHER * t, TOGETHER)

    def core_sum(t):
        return remote(
            part.at[1 - core, span(t)], from_core.at[span(t)],
            sum_core_send.at[t], sum_core_recv.at[t], core_dev,
        )

    def x_sum(t):
        return remote(
            to_x.at[span(t)], from_x.at[span(t)], sum_x_send.at[t], sum_x_recv.at[t], x_dev
        )

    def send_sum(t):
        core_sum(t).wait_recv()
        total = part[core, span(t), 1 - x].astype(jnp.float32)
        total = total + from_core[span(t), 1 - x].astype(jnp.float32)
        to_x[span(t)] = total.astype(jnp.bfloat16)
        x_sum(t).start()

    quarter = BLOCK_SIDE // 4
    first = (((0,), (0,)), ((), ()))

    def column_inputs(g, rows_of):
        ids = [ids_ref[BLOCKS_PER_COLUMN * g + i] for i in range(BLOCKS_PER_COLUMN)]
        x_cat = jnp.concatenate([rows_of(r) for r in ids], axis=1)
        g_cat = jnp.concatenate([rows_of(n_rows + r) for r in ids], axis=1)
        slots = pl.ds(BLOCKS_PER_COLUMN * g, BLOCKS_PER_COLUMN)
        w_rows = w_in[slots].reshape(BLOCKS_PER_COLUMN * BLOCK_SIDE, BLOCK_SIDE)
        wo = w_out[slots]
        w_cols = jnp.concatenate([wo[i] for i in range(BLOCKS_PER_COLUMN)], axis=1)
        pre_act = jnp.dot(x_cat, w_rows, preferred_element_type=jnp.float32)
        grad_act = lax.dot_general(
            g_cat, w_cols, (((1,), (1,)), ((), ())), preferred_element_type=jnp.float32
        )
        return x_cat, g_cat, pre_act, grad_act

    def column_grads(store, g, x_cat, g_cat, pre_act, grad_act):
        activation, gelu_slope = gelu_pair(pre_act)
        activation = activation.astype(jnp.bfloat16)
        grad_pre = (grad_act * gelu_slope).astype(jnp.bfloat16)
        share_in = lax.dot_general(grad_pre, x_cat, first, preferred_element_type=jnp.float32)
        share_out = lax.dot_general(activation, g_cat, first, preferred_element_type=jnp.float32)
        share_in = share_in.astype(jnp.bfloat16)
        share_out = share_out.astype(jnp.bfloat16)
        for i in range(BLOCKS_PER_COLUMN):
            cols = slice(i * BLOCK_SIDE, (i + 1) * BLOCK_SIDE)
            two = (share_in[:, cols].T, share_out[:, cols])
            for a in range(2):
                for q in range(4):
                    store(q % 2, q // 2, g, a, i, two[a][q * quarter : (q + 1) * quarter])

    def columns_of(t, rows_of, store):
        columns = [TOGETHER * t + u for u in range(TOGETHER)]
        held = [column_inputs(g, rows_of) for g in columns]
        for g, values in zip(columns, held):
            column_grads(store, g, *values)

    def solo_rows(r):
        return feat[r]

    def solo_store(to_core, to_chip, g, a, i, value):
        part[to_core, g, to_chip, a, i] = value

    def shared_rows(r):
        return feat_shared[r].reshape(2 * origin, BLOCK_SIDE)

    def shared_store(to_core, to_chip, g, a, i, value):
        part_shared[to_core, to_chip, g, a, i] = value

    n_pass = (NZ - 1) * pieces

    def turn_columns(t, carry):
        columns_of(t, solo_rows, solo_store)
        core_sum(t).start()
        lax.fori_loop(n_pass * t // turns, n_pass * (t + 1) // turns, pass_shared, 0)

        @pl.when(t > 0)
        def _():
            send_sum(t - 1)

        return carry

    lax.fori_loop(0, turns, turn_columns, 0)
    send_sum(turns - 1)

    def end_shared(p, carry):
        for source_z in range(NZ):
            shared_y(source_z, 1 - y, p).wait_recv()
        return carry

    lax.fori_loop(0, pieces, end_shared, 0)

    def shared_sum(t):
        return remote(
            part_shared.at[1 - core, x, span(t)], shared_core.at[span(t)],
            sc_send.at[t], sc_recv.at[t], core_dev,
        )

    per_turn = TOGETHER * BLOCKS_PER_COLUMN

    def stores(t):
        at = pl.ds(per_turn * t, per_turn)
        return [
            pltpu.make_async_copy(staged.at[a, at], ref.at[at], store_sem.at[a, t])
            for a, ref in enumerate((out_in_ref, out_out_ref))
        ]

    def finish(t):
        shared_sum(t).wait_recv()
        x_sum(t).wait_recv()
        total = (
            part[core, span(t), x].astype(jnp.float32)
            + from_core[span(t), x].astype(jnp.float32)
            + from_x[span(t)].astype(jnp.float32)
            + part_shared[core, x, span(t)].astype(jnp.float32)
            + shared_core[span(t)].astype(jnp.float32)
        ).astype(jnp.bfloat16)
        for u in range(TOGETHER):
            at = pl.ds(per_turn * t + u * BLOCKS_PER_COLUMN, BLOCKS_PER_COLUMN)
            for a in range(2):
                staged[a, at] = total[u, a]
        for store in stores(t):
            store.start()

    def turn_shared(t, carry):
        columns_of(t, shared_rows, shared_store)
        shared_sum(t).start()

        @pl.when(t > 0)
        def _():
            finish(t - 1)

        return carry

    lax.fori_loop(0, turns, turn_shared, 0)
    finish(turns - 1)

    def end_sums(t, carry):
        core_sum(t).wait_send()
        x_sum(t).wait_send()
        shared_sum(t).wait_send()
        for store in stores(t):
            store.wait()
        return carry

    lax.fori_loop(0, turns, end_sums, 0)

    def end_sends(other, late, across):
        def body(p, carry):
            for source_z in range(NZ):
                if across:
                    if not other:
                        @pl.when(source_z == z)
                        def _():
                            y_copy(source_z, y, late, p).wait_send()
                else:
                    y_copy(source_z, y, late, p).wait_send()

                @pl.when(jnp.logical_and(z < NZ - 1, source_z <= z))
                def _():
                    z_copy(True, source_z, other, late, p).wait_send()

                @pl.when(jnp.logical_and(z > 0, source_z >= z))
                def _():
                    z_copy(False, source_z, other, late, p).wait_send()

            return carry

        return body

    lax.fori_loop(0, ACROSS, end_sends(False, False, True), 0)
    lax.fori_loop(ACROSS, pieces, end_sends(False, False, False), 0)
    lax.fori_loop(0, ACROSS, end_sends(True, False, True), 0)
    lax.fori_loop(0, pieces, end_sends(False, True, False), 0)

    def end_shared_sends(p, carry):
        for source_z in range(NZ):
            shared_y(source_z, y, p).wait_send()

            @pl.when(jnp.logical_and(z < NZ - 1, source_z <= z))
            def _():
                shared_z(True, source_z, p).wait_send()

            @pl.when(jnp.logical_and(z > 0, source_z >= z))
            def _():
                shared_z(False, source_z, p).wait_send()

        return carry

    lax.fori_loop(0, pieces, end_shared_sends, 0)


def deliver_kernel(in_ref, out_ref, in_final, out_final, held, sems):
    pairs = []
    for a, (source, target) in enumerate(((in_ref, in_final), (out_ref, out_final))):
        step = source.shape[0] // DELIVERY_PARTS
        for k in range(DELIVERY_PARTS):
            at = pl.ds(k * step, step)
            pairs.append((
                pltpu.make_async_copy(source.at[at], held.at[a, at], sems.at[0, a, k]),
                pltpu.make_async_copy(held.at[a, at], target.at[at], sems.at[1, a, k]),
            ))
    for load, store in pairs:
        load.start()
    for load, store in pairs:
        load.wait()
        store.start()
    for load, store in pairs:
        store.wait()


def packed_shards(tokens, grad_out, input_weight_blocks, output_weight_blocks, row_ids, lengths):
    rows, width = tokens.shape
    slots = input_weight_blocks.shape[0]
    groups = slots // BLOCKS_PER_COLUMN
    n_blk, n_seq = PLAN_MESH
    keep = rows * 5 // 8
    spare = rows - keep
    origin = keep // 5
    solo = keep - origin
    turns = groups // TOGETHER
    n_rows = n_blk * width // BLOCK_SIDE
    pieces = 2 * width // BLOCK_SIDE
    quarter = BLOCK_SIDE // n_seq
    sums = (2, BLOCKS_PER_COLUMN, quarter, BLOCK_SIDE)
    bf16 = jnp.bfloat16
    dma = pltpu.SemaphoreType.DMA
    any_spec = pl.BlockSpec(memory_space=pl.ANY)
    smem = pl.BlockSpec(memory_space=pltpu.SMEM)
    out = jax.ShapeDtypeStruct((slots, quarter, BLOCK_SIDE), bf16)
    parts = pl.pallas_call(
        pack_gather_grad_kernel,
        out_shape=(out, out),
        in_specs=[any_spec] * 4 + [smem] * 2,
        out_specs=(any_spec, any_spec),
        scratch_shapes=[
            pltpu.VMEM((2, 2, rows, width), bf16),
            pltpu.VMEM((2, 8, 128), jnp.int32),
            pltpu.VMEM((2, spare, width), bf16),
            pltpu.VMEM((2, spare, width), bf16),
            pltpu.VMEM((2 * n_rows, solo, BLOCK_SIDE), bf16),
            pltpu.VMEM((slots, BLOCK_SIDE, BLOCK_SIDE), bf16),
            pltpu.VMEM((slots, BLOCK_SIDE, BLOCK_SIDE), bf16),
            pltpu.VMEM((2, groups, 2) + sums, bf16),
            pltpu.VMEM((groups, 2) + sums, bf16),
            pltpu.VMEM((groups,) + sums, bf16),
            pltpu.VMEM((groups,) + sums, bf16),
            pltpu.VMEM((2, slots, quarter, BLOCK_SIDE), bf16),
            pltpu.VMEM((2 * n_rows, 2, origin, BLOCK_SIDE), bf16),
            pltpu.VMEM((2, 2, groups) + sums, bf16),
            pltpu.VMEM((groups,) + sums, bf16),
            dma((4,)),
            dma((5,)),
            dma((5,)),
            dma((2,)),
            dma((2,)),
            dma((2, NZ, 2 * pieces + ACROSS)),
            dma((NZ, 2 * pieces + ACROSS)),
            dma((NZ, 2 * pieces)),
            dma((NZ, 2 * pieces)),
            dma((turns,)),
            dma((turns,)),
            dma((turns,)),
            dma((turns,)),
            dma((2, turns)),
            dma((2, NZ, pieces)),
            dma((NZ, pieces)),
            dma((NZ, pieces)),
            dma((NZ, pieces)),
            dma((2,)),
            dma((2,)),
            dma((turns,)),
            dma((turns,)),
        ],
        compiler_params=pltpu.CompilerParams(
            collective_id=0, has_side_effects=True, vmem_limit_bytes=60 * 1024 * 1024
        ),
    )(tokens, grad_out, input_weight_blocks, output_weight_blocks, row_ids, lengths)
    return pl.pallas_call(
        deliver_kernel,
        out_shape=(out, out),
        in_specs=[any_spec] * 2,
        out_specs=(any_spec, any_spec),
        scratch_shapes=[
            pltpu.VMEM((2, slots, quarter, BLOCK_SIDE), bf16),
            dma((2, 2, DELIVERY_PARTS)),
        ],
        compiler_params=pltpu.CompilerParams(vmem_limit_bytes=60 * 1024 * 1024),
    )(*parts)


def solution(mesh):
    return jax.shard_map(
        packed_shards if tuple(mesh.shape.values()) == PLAN_MESH else shards,
        mesh=mesh,
        in_specs=(
            P("seq", "blk"),
            P("seq", "blk"),
            P("blk", None, None),
            P("blk", None, None),
            P("blk"),
            P("seq"),
        ),
        out_specs=(P("blk", "seq", None), P("blk", "seq", None)),
        check_vma=False,
    )
```

```python
import jax
import jax.numpy as jnp
from jax import lax
from jax.experimental import pallas as pl
from jax.experimental.pallas import tpu as pltpu
from jax.sharding import PartitionSpec as P

BLOCK_SIDE = 128
BLOCKS_PER_COLUMN = 4


gelu_scale = 0.7978845608


def gelu_pair(pre_act):
    tanh_val = jnp.tanh(gelu_scale * (pre_act + 0.044715 * pre_act * pre_act * pre_act))
    activation = 0.5 * pre_act * (1.0 + tanh_val)
    gelu_slope = 0.5 * (1.0 + tanh_val) + 0.5 * pre_act * (
        1.0 - tanh_val * tanh_val
    ) * gelu_scale * (1.0 + 0.134145 * pre_act * pre_act)
    return (activation, gelu_slope)


def shards(tokens, grad_out, input_weight_blocks, output_weight_blocks, row_ids, lengths):
    tok_rows = tokens.shape[0]
    groups = input_weight_blocks.shape[0] // BLOCKS_PER_COLUMN
    live_rows = lax.iota(jnp.int32, tok_rows)[:, None] < lengths[0]
    masked = jnp.where(live_rows, grad_out, jnp.zeros_like(grad_out))
    features = lax.all_gather(tokens, "blk", axis=1, tiled=True)
    x_slots = features.reshape(tok_rows, -1, BLOCK_SIDE)[:, row_ids, :]
    pre_slot = jnp.einsum(
        "tkc,kch->tkh", x_slots, input_weight_blocks, preferred_element_type=jnp.float32
    )
    pre_act = pre_slot.reshape(tok_rows, groups, BLOCKS_PER_COLUMN, BLOCK_SIDE).sum(2)
    activation, gelu_slope = gelu_pair(pre_act)
    activation = activation.astype(jnp.bfloat16)
    gradient = lax.all_gather(masked, "blk", axis=1, tiled=True)
    gradient_slots = gradient.reshape(tok_rows, -1, BLOCK_SIDE)[:, row_ids, :]
    g_four = gradient_slots.reshape(tok_rows, groups, BLOCKS_PER_COLUMN, BLOCK_SIDE)
    output_share = jnp.einsum(
        "tgh,tgrf->grhf", activation, g_four, preferred_element_type=jnp.float32
    )
    output_share = output_share.reshape(-1, BLOCK_SIDE, BLOCK_SIDE)
    slot_gradient = jnp.einsum(
        "xcn,cpn->xcp", gradient_slots, output_weight_blocks, preferred_element_type=jnp.float32
    )
    grad_act = slot_gradient.reshape(tok_rows, groups, BLOCKS_PER_COLUMN, BLOCK_SIDE).sum(2)
    grad_pre = (grad_act * gelu_slope).astype(jnp.bfloat16)
    x_four = x_slots.reshape(tok_rows, groups, BLOCKS_PER_COLUMN, BLOCK_SIDE)
    input_share = jnp.einsum("tgrc,tgh->grch", x_four, grad_pre, preferred_element_type=jnp.float32)
    input_share = input_share.reshape(-1, BLOCK_SIDE, BLOCK_SIDE)
    in_total, out_total = (
        lax.psum_scatter(
            input_share.astype(jnp.bfloat16), "seq", scatter_dimension=1, tiled=True
        ).astype(jnp.float32),
        lax.psum_scatter(
            output_share.astype(jnp.bfloat16), "seq", scatter_dimension=1, tiled=True
        ).astype(jnp.float32),
    )
    return (in_total.astype(jnp.bfloat16), out_total.astype(jnp.bfloat16))


PLAN_MESH = (8, 4)
NZ = 4
ACROSS = 3
TOGETHER = 2
DELIVERY_PARTS = 4
MESH = pl.DeviceIdType.MESH


def pack_gather_grad_kernel(
    tokens_ref, grad_ref, w_in_ref, w_out_ref, ids_ref, len_ref, out_in_ref, out_out_ref,
    chip, lens, give, got, feat, w_in, w_out, part, from_core, to_x, from_x, staged,
    feat_shared, part_shared, shared_core, mid,
    load_sem, core_send, core_recv, x_send, x_recv, z_send, z_recv, y_send, y_recv,
    sum_core_send, sum_core_recv, sum_x_send, sum_x_recv, store_sem,
    sz_send, sz_recv, sy_send, sy_recv, sx_send, sx_recv, sc_send, sc_recv,
):
    rows = chip.shape[2]
    width = chip.shape[3]
    solo = feat.shape[1]
    origin = feat_shared.shape[2]
    keep = solo + origin
    spare = got.shape[1]
    per = width // BLOCK_SIDE
    n_rows = feat.shape[0] // 2
    groups = part.shape[1]
    pieces = 2 * per
    early = rows - 2 * spare
    head = 2 * early
    halves = (pl.ds(0, head), pl.ds(head, rows - head))

    blk = lax.axis_index("blk")
    seq = lax.axis_index("seq")
    z, y = blk // 2, blk % 2
    x, core = seq // 2, seq % 2
    core_dev = {"seq": seq + 1 - 2 * core}
    x_dev = {"seq": seq + 2 - 4 * x}
    y_dev = {"blk": blk + 1 - 2 * y}
    up_dev = {"blk": blk + 2}
    down_dev = {"blk": blk - 2}

    def remote(src, dst, send, recv, device):
        return pltpu.make_async_remote_copy(
            src_ref=src, dst_ref=dst, send_sem=send, recv_sem=recv,
            device_id=device, device_id_type=MESH,
        )

    barrier = pltpu.get_barrier_semaphore()
    for device in (core_dev, x_dev, y_dev):
        pl.semaphore_signal(barrier, inc=1, device_id=device, device_id_type=MESH)

    @pl.when(z > 0)
    def _():
        pl.semaphore_signal(barrier, inc=1, device_id=down_dev, device_id_type=MESH)

    @pl.when(z < NZ - 1)
    def _():
        pl.semaphore_signal(barrier, inc=1, device_id=up_dev, device_id_type=MESH)

    own_loads = [
        pltpu.make_async_copy(ref, chip.at[a, core], load_sem.at[a])
        for a, ref in enumerate((tokens_ref, grad_ref))
    ]
    weight_loads = [
        pltpu.make_async_copy(w_in_ref, w_in, load_sem.at[2]),
        pltpu.make_async_copy(w_out_ref, w_out, load_sem.at[3]),
    ]
    for load in own_loads:
        load.start()
    lens[core] = jnp.full(lens.shape[1:], len_ref[0], jnp.int32)
    pl.semaphore_wait(barrier, 3 + jnp.where(z > 0, 1, 0) + jnp.where(z < NZ - 1, 1, 0))

    len_swap = remote(lens.at[core], lens.at[core], core_send.at[4], core_recv.at[4], core_dev)
    len_swap.start()
    swaps = [
        [
            remote(
                ref.at[half], chip.at[a, core, half],
                core_send.at[2 * h + a], core_recv.at[2 * h + a], core_dev,
            )
            for a, ref in enumerate((tokens_ref, grad_ref))
        ]
        for h, half in enumerate(halves)
    ]
    for swap in swaps[0] + swaps[1]:
        swap.start()
    len_swap.wait()
    len_a = lens[0][0:1, 0:1]
    len_b = lens[1][0:1, 0:1]
    count = len_a + len_b

    def places(held):
        row = lax.broadcasted_iota(jnp.int32, (1, 2 * held), 1)
        return jnp.where(
            row < held,
            jnp.where(row < len_a, row, -1),
            jnp.where(row - held < len_b, row - held + len_a, -1),
        )

    place = places(rows)
    odd_give = jnp.bitwise_and(4 * keep - count + core, 1)
    odd_got = jnp.bitwise_and(count + core, 1)
    keep_at = 2 * lax.broadcasted_iota(jnp.int32, (keep, 1), 0) + core
    give_at = 2 * keep + odd_give + 2 * lax.broadcasted_iota(jnp.int32, (spare, 1), 0)
    got_at = count + odd_got + 2 * lax.broadcasted_iota(jnp.int32, (1, spare), 1)
    one, zero = jnp.float32(1), jnp.float32(0)
    pick_early = jnp.where(places(head) == keep_at[:early], one, zero).astype(jnp.bfloat16)
    pick_late = jnp.where(place == keep_at[early:], one, zero).astype(jnp.bfloat16)
    pick_give = jnp.where(place == give_at, one, zero).astype(jnp.bfloat16)
    pick_got = jnp.where(got_at == keep_at[early:], one, zero).astype(jnp.bfloat16)

    def feat_piece(source, late, p):
        at = feat.at[(p // per) * n_rows + per * source + p % per]
        return at.at[pl.ds(early, solo - early)] if late else at.at[pl.ds(0, early)]

    def z_copy(up, source_z, other, late, p, recv_only=False):
        ref = feat_piece(2 * source_z + (1 - y if other else y), late, p)
        slot = p + (2 * pieces if other else pieces if late else 0)
        return remote(
            ref, ref, z_send.at[0 if up else 1, source_z, slot], z_recv.at[source_z, slot],
            y_dev if recv_only else (up_dev if up else down_dev),
        )

    def y_copy(source_z, source_y, late, p):
        ref = feat_piece(2 * source_z + source_y, late, p)
        slot = p + (pieces if late else 0)
        return remote(ref, ref, y_send.at[source_z, slot], y_recv.at[source_z, slot], y_dev)

    def z_both(other, late, p):
        @pl.when(z < NZ - 1)
        def _():
            z_copy(True, z, other, late, p).start()

        @pl.when(z > 0)
        def _():
            z_copy(False, z, other, late, p).start()

    def send_own(late, a):
        def body(i, carry):
            p = a * per + i
            z_both(False, late, p)
            y_copy(z, y, late, p).start()
            return carry

        lax.fori_loop(0, per, body, 0)

    def pass_on(step, late, own=True, others=True):
        below = z - 1 - step
        above = z + 1 + step

        def arrivals(other, across):
            def body(p, carry):
                @pl.when(below >= 0)
                def _():
                    z_copy(True, below, other, late, p, recv_only=True).wait_recv()

                    @pl.when(z < NZ - 1)
                    def _():
                        z_copy(True, below, other, late, p).start()

                    if not across:
                        y_copy(below, y, late, p).start()

                @pl.when(above < NZ)
                def _():
                    z_copy(False, above, other, late, p, recv_only=True).wait_recv()

                    @pl.when(z > 0)
                    def _():
                        z_copy(False, above, other, late, p).start()

                    if not across:
                        y_copy(above, y, late, p).start()

                return carry

            return body

        if late:
            lax.fori_loop(0, pieces, arrivals(False, False), 0)
        if own and not late:
            lax.fori_loop(0, ACROSS, arrivals(False, True), 0)
            lax.fori_loop(ACROSS, pieces, arrivals(False, False), 0)
        if others and not late:
            lax.fori_loop(0, ACROSS, arrivals(True, True), 0)

    def both(a):
        return chip[a].reshape(2 * rows, width)

    def place_block(block, first, a):
        block = block.astype(jnp.bfloat16)
        for i in range(per):
            feat[a * n_rows + per * blk + i, first : first + block.shape[0]] = block[
                :, i * BLOCK_SIDE : (i + 1) * BLOCK_SIDE
            ]

    def share_x(a):
        ref = feat_shared.at[pl.ds(a * n_rows + per * blk, per), x]
        return remote(ref, ref, sx_send.at[a], sx_recv.at[a], x_dev)

    def shared_piece(source, p):
        return feat_shared.at[(p // per) * n_rows + per * source + p % per]

    def shared_z(up, source_z, p, recv_only=False):
        ref = shared_piece(2 * source_z + y, p)
        return remote(
            ref, ref, sz_send.at[0 if up else 1, source_z, p], sz_recv.at[source_z, p],
            y_dev if recv_only else (up_dev if up else down_dev),
        )

    def shared_y(source_z, source_y, p):
        ref = shared_piece(2 * source_z + source_y, p)
        return remote(ref, ref, sy_send.at[source_z, p], sy_recv.at[source_z, p], y_dev)

    def send_shared(p, carry):
        shared_y(z, y, p).start()

        @pl.when(z < NZ - 1)
        def _():
            shared_z(True, z, p).start()

        @pl.when(z > 0)
        def _():
            shared_z(False, z, p).start()

        return carry

    def pass_shared(k, carry):
        step, p = k // pieces, k % pieces
        below = z - 1 - step
        above = z + 1 + step

        @pl.when(below >= 0)
        def _():
            shared_z(True, below, p, recv_only=True).wait_recv()

            @pl.when(z < NZ - 1)
            def _():
                shared_z(True, below, p).start()

            shared_y(below, y, p).start()

        @pl.when(above < NZ)
        def _():
            shared_z(False, above, p, recv_only=True).wait_recv()

            @pl.when(z > 0)
            def _():
                shared_z(False, above, p).start()

            shared_y(above, y, p).start()

        return carry

    for a in range(2):
        own_loads[a].wait()
        swaps[0][a].wait()
        heads = chip[a, :, :head].reshape(2 * head, width)
        place_block(jnp.dot(pick_early, heads, preferred_element_type=jnp.float32), 0, a)
        send_own(False, a)
    for load in weight_loads:
        load.start()
    x_moves = []
    for a in range(2):
        swaps[1][a].wait()
        give[a] = jnp.dot(pick_give, both(a), preferred_element_type=jnp.float32).astype(jnp.bfloat16)
        move = remote(give.at[a], got.at[a], x_send.at[a], x_recv.at[a], x_dev)
        move.start()
        x_moves.append(move)
    for a in range(2):
        mid[a] = jnp.dot(pick_late, both(a), preferred_element_type=jnp.float32).astype(jnp.bfloat16)

    def turn(p, carry):
        y_copy(z, 1 - y, False, p).wait_recv()
        z_both(True, False, p)
        return carry

    lax.fori_loop(0, ACROSS, turn, 0)
    pass_on(0, False)
    pass_on(1, False, others=False)
    for a in range(2):
        x_moves[a].wait()
        kept = mid[a].astype(jnp.float32) + jnp.dot(pick_got, got[a], preferred_element_type=jnp.float32)
        place_block(kept[: solo - early], early, a)
        send_own(True, a)
        last = kept[solo - early :].astype(jnp.bfloat16)
        for i in range(per):
            feat_shared[a * n_rows + per * blk + i, x] = last[
                :, i * BLOCK_SIDE : (i + 1) * BLOCK_SIDE
            ]
        share_x(a).start()
    pass_on(1, False, own=False)
    pass_on(0, True)
    pass_on(2, False)
    pass_on(1, True)
    pass_on(2, True)
    for a in range(2):
        share_x(a).wait()
    lax.fori_loop(0, pieces, send_shared, 0)

    def end_early(p, carry):
        for source_z in range(NZ):
            y_copy(source_z, 1 - y, False, p).wait_recv()
        return carry

    def end_late(p, carry):
        for source_z in range(NZ):
            y_copy(source_z, 1 - y, True, p).wait_recv()
        return carry

    lax.fori_loop(ACROSS, pieces, end_early, 0)
    lax.fori_loop(0, pieces, end_late, 0)

    for load in weight_loads:
        load.wait()

    def core_sum(g):
        return remote(
            part.at[1 - core, g], from_core.at[g], sum_core_send.at[g], sum_core_recv.at[g], core_dev
        )

    def x_sum(g):
        return remote(to_x.at[g], from_x.at[g], sum_x_send.at[g], sum_x_recv.at[g], x_dev)

    def send_sum(g):
        core_sum(g).wait_recv()
        total = part[core, g, 1 - x].astype(jnp.float32) + from_core[g, 1 - x].astype(jnp.float32)
        to_x[g] = total.astype(jnp.bfloat16)
        x_sum(g).start()

    turns = groups // TOGETHER

    def span(t):
        return pl.ds(TOGETHER * t, TOGETHER)

    quarter = BLOCK_SIDE // 4
    first = (((0,), (0,)), ((), ()))

    def column_inputs(g, rows_of):
        ids = [ids_ref[BLOCKS_PER_COLUMN * g + i] for i in range(BLOCKS_PER_COLUMN)]
        x_cat = jnp.concatenate([rows_of(r) for r in ids], axis=1)
        g_cat = jnp.concatenate([rows_of(n_rows + r) for r in ids], axis=1)
        slots = pl.ds(BLOCKS_PER_COLUMN * g, BLOCKS_PER_COLUMN)
        w_rows = w_in[slots].reshape(BLOCKS_PER_COLUMN * BLOCK_SIDE, BLOCK_SIDE)
        wo = w_out[slots]
        w_cols = jnp.concatenate([wo[i] for i in range(BLOCKS_PER_COLUMN)], axis=1)
        pre_act = jnp.dot(x_cat, w_rows, preferred_element_type=jnp.float32)
        grad_act = lax.dot_general(
            g_cat, w_cols, (((1,), (1,)), ((), ())), preferred_element_type=jnp.float32
        )
        return x_cat, g_cat, pre_act, grad_act

    def column_grads(store, g, x_cat, g_cat, pre_act, grad_act):
        activation, gelu_slope = gelu_pair(pre_act)
        activation = activation.astype(jnp.bfloat16)
        grad_pre = (grad_act * gelu_slope).astype(jnp.bfloat16)
        share_in = lax.dot_general(grad_pre, x_cat, first, preferred_element_type=jnp.float32)
        share_out = lax.dot_general(activation, g_cat, first, preferred_element_type=jnp.float32)
        share_in = share_in.astype(jnp.bfloat16)
        share_out = share_out.astype(jnp.bfloat16)
        for i in range(BLOCKS_PER_COLUMN):
            cols = slice(i * BLOCK_SIDE, (i + 1) * BLOCK_SIDE)
            two = (share_in[:, cols].T, share_out[:, cols])
            for a in range(2):
                for q in range(4):
                    store(q % 2, q // 2, g, a, i, two[a][q * quarter : (q + 1) * quarter])

    def columns_of(columns, rows_of, store):
        held = [column_inputs(g, rows_of) for g in columns]
        for g, values in zip(columns, held):
            column_grads(store, g, *values)

    def solo_rows(r):
        return feat[r]

    def solo_store(to_core, to_chip, g, a, i, value):
        part[to_core, g, to_chip, a, i] = value

    def shared_rows(r):
        return feat_shared[r].reshape(2 * origin, BLOCK_SIDE)

    def shared_store(to_core, to_chip, g, a, i, value):
        part_shared[to_core, to_chip, g, a, i] = value

    n_pass = (NZ - 1) * pieces

    def solo_column(g, carry):
        columns_of([g], solo_rows, solo_store)
        core_sum(g).start()

        @pl.when(g > 0)
        def _():
            send_sum(g - 1)

        lax.fori_loop(n_pass * g // groups, n_pass * (g + 1) // groups, pass_shared, 0)
        return carry

    lax.fori_loop(0, groups, solo_column, 0)
    send_sum(groups - 1)

    def end_shared(p, carry):
        for source_z in range(NZ):
            shared_y(source_z, 1 - y, p).wait_recv()
        return carry

    lax.fori_loop(0, pieces, end_shared, 0)

    def shared_sum(t):
        return remote(
            part_shared.at[1 - core, x, span(t)], shared_core.at[span(t)],
            sc_send.at[t], sc_recv.at[t], core_dev,
        )

    per_turn = TOGETHER * BLOCKS_PER_COLUMN

    def stores(t):
        at = pl.ds(per_turn * t, per_turn)
        return [
            pltpu.make_async_copy(staged.at[a, at], ref.at[at], store_sem.at[a, t])
            for a, ref in enumerate((out_in_ref, out_out_ref))
        ]

    def finish(t):
        shared_sum(t).wait_recv()
        for u in range(TOGETHER):
            x_sum(TOGETHER * t + u).wait_recv()
        total = (
            part[core, span(t), x].astype(jnp.float32)
            + from_core[span(t), x].astype(jnp.float32)
            + from_x[span(t)].astype(jnp.float32)
            + part_shared[core, x, span(t)].astype(jnp.float32)
            + shared_core[span(t)].astype(jnp.float32)
        ).astype(jnp.bfloat16)
        for u in range(TOGETHER):
            at = pl.ds(per_turn * t + u * BLOCKS_PER_COLUMN, BLOCKS_PER_COLUMN)
            for a in range(2):
                staged[a, at] = total[u, a]
        for store in stores(t):
            store.start()

    def turn_shared(t, carry):
        columns_of([TOGETHER * t + u for u in range(TOGETHER)], shared_rows, shared_store)
        shared_sum(t).start()

        @pl.when(t > 0)
        def _():
            finish(t - 1)

        return carry

    lax.fori_loop(0, turns, turn_shared, 0)
    finish(turns - 1)

    def end_sums(t, carry):
        for u in range(TOGETHER):
            core_sum(TOGETHER * t + u).wait_send()
            x_sum(TOGETHER * t + u).wait_send()
        shared_sum(t).wait_send()
        for store in stores(t):
            store.wait()
        return carry

    lax.fori_loop(0, turns, end_sums, 0)

    def end_sends(other, late, across):
        def body(p, carry):
            for source_z in range(NZ):
                if across:
                    if not other:
                        @pl.when(source_z == z)
                        def _():
                            y_copy(source_z, y, late, p).wait_send()
                else:
                    y_copy(source_z, y, late, p).wait_send()

                @pl.when(jnp.logical_and(z < NZ - 1, source_z <= z))
                def _():
                    z_copy(True, source_z, other, late, p).wait_send()

                @pl.when(jnp.logical_and(z > 0, source_z >= z))
                def _():
                    z_copy(False, source_z, other, late, p).wait_send()

            return carry

        return body

    lax.fori_loop(0, ACROSS, end_sends(False, False, True), 0)
    lax.fori_loop(ACROSS, pieces, end_sends(False, False, False), 0)
    lax.fori_loop(0, ACROSS, end_sends(True, False, True), 0)
    lax.fori_loop(0, pieces, end_sends(False, True, False), 0)

    def end_shared_sends(p, carry):
        for source_z in range(NZ):
            shared_y(source_z, y, p).wait_send()

            @pl.when(jnp.logical_and(z < NZ - 1, source_z <= z))
            def _():
                shared_z(True, source_z, p).wait_send()

            @pl.when(jnp.logical_and(z > 0, source_z >= z))
            def _():
                shared_z(False, source_z, p).wait_send()

        return carry

    lax.fori_loop(0, pieces, end_shared_sends, 0)


def deliver_kernel(in_ref, out_ref, in_final, out_final, held, sems):
    pairs = []
    for a, (source, target) in enumerate(((in_ref, in_final), (out_ref, out_final))):
        step = source.shape[0] // DELIVERY_PARTS
        for k in range(DELIVERY_PARTS):
            at = pl.ds(k * step, step)
            pairs.append((
                pltpu.make_async_copy(source.at[at], held.at[a, at], sems.at[0, a, k]),
                pltpu.make_async_copy(held.at[a, at], target.at[at], sems.at[1, a, k]),
            ))
    for load, store in pairs:
        load.start()
    for load, store in pairs:
        load.wait()
        store.start()
    for load, store in pairs:
        store.wait()


def packed_shards(tokens, grad_out, input_weight_blocks, output_weight_blocks, row_ids, lengths):
    rows, width = tokens.shape
    slots = input_weight_blocks.shape[0]
    groups = slots // BLOCKS_PER_COLUMN
    n_blk, n_seq = PLAN_MESH
    keep = rows * 5 // 8
    spare = rows - keep
    origin = keep // 5
    solo = keep - origin
    turns = groups // TOGETHER
    n_rows = n_blk * width // BLOCK_SIDE
    pieces = 2 * width // BLOCK_SIDE
    quarter = BLOCK_SIDE // n_seq
    sums = (2, BLOCKS_PER_COLUMN, quarter, BLOCK_SIDE)
    bf16 = jnp.bfloat16
    dma = pltpu.SemaphoreType.DMA
    any_spec = pl.BlockSpec(memory_space=pl.ANY)
    smem = pl.BlockSpec(memory_space=pltpu.SMEM)
    out = jax.ShapeDtypeStruct((slots, quarter, BLOCK_SIDE), bf16)
    parts = pl.pallas_call(
        pack_gather_grad_kernel,
        out_shape=(out, out),
        in_specs=[any_spec] * 4 + [smem] * 2,
        out_specs=(any_spec, any_spec),
        scratch_shapes=[
            pltpu.VMEM((2, 2, rows, width), bf16),
            pltpu.VMEM((2, 8, 128), jnp.int32),
            pltpu.VMEM((2, spare, width), bf16),
            pltpu.VMEM((2, spare, width), bf16),
            pltpu.VMEM((2 * n_rows, solo, BLOCK_SIDE), bf16),
            pltpu.VMEM((slots, BLOCK_SIDE, BLOCK_SIDE), bf16),
            pltpu.VMEM((slots, BLOCK_SIDE, BLOCK_SIDE), bf16),
            pltpu.VMEM((2, groups, 2) + sums, bf16),
            pltpu.VMEM((groups, 2) + sums, bf16),
            pltpu.VMEM((groups,) + sums, bf16),
            pltpu.VMEM((groups,) + sums, bf16),
            pltpu.VMEM((2, slots, quarter, BLOCK_SIDE), bf16),
            pltpu.VMEM((2 * n_rows, 2, origin, BLOCK_SIDE), bf16),
            pltpu.VMEM((2, 2, groups) + sums, bf16),
            pltpu.VMEM((groups,) + sums, bf16),
            pltpu.VMEM((2, spare, width), bf16),
            dma((4,)),
            dma((5,)),
            dma((5,)),
            dma((2,)),
            dma((2,)),
            dma((2, NZ, 2 * pieces + ACROSS)),
            dma((NZ, 2 * pieces + ACROSS)),
            dma((NZ, 2 * pieces)),
            dma((NZ, 2 * pieces)),
            dma((groups,)),
            dma((groups,)),
            dma((groups,)),
            dma((groups,)),
            dma((2, turns)),
            dma((2, NZ, pieces)),
            dma((NZ, pieces)),
            dma((NZ, pieces)),
            dma((NZ, pieces)),
            dma((2,)),
            dma((2,)),
            dma((turns,)),
            dma((turns,)),
        ],
        compiler_params=pltpu.CompilerParams(
            collective_id=0, has_side_effects=True, vmem_limit_bytes=60 * 1024 * 1024
        ),
    )(tokens, grad_out, input_weight_blocks, output_weight_blocks, row_ids, lengths)
    return pl.pallas_call(
        deliver_kernel,
        out_shape=(out, out),
        in_specs=[any_spec] * 2,
        out_specs=(any_spec, any_spec),
        scratch_shapes=[
            pltpu.VMEM((2, slots, quarter, BLOCK_SIDE), bf16),
            dma((2, 2, DELIVERY_PARTS)),
        ],
        compiler_params=pltpu.CompilerParams(vmem_limit_bytes=60 * 1024 * 1024),
    )(*parts)


def solution(mesh):
    return jax.shard_map(
        packed_shards if tuple(mesh.shape.values()) == PLAN_MESH else shards,
        mesh=mesh,
        in_specs=(
            P("seq", "blk"),
            P("seq", "blk"),
            P("blk", None, None),
            P("blk", None, None),
            P("blk"),
            P("seq"),
        ),
        out_specs=(P("blk", "seq", None), P("blk", "seq", None)),
        check_vma=False,
    )
```

```python
import jax
import jax.numpy as jnp
from jax import lax
from jax.experimental import pallas as pl
from jax.experimental.pallas import tpu as pltpu
from jax.sharding import PartitionSpec as P

BLOCK_SIDE = 128
BLOCKS_PER_COLUMN = 4


gelu_scale = 0.7978845608


def gelu_pair(pre_act):
    tanh_val = jnp.tanh(gelu_scale * (pre_act + 0.044715 * pre_act * pre_act * pre_act))
    activation = 0.5 * pre_act * (1.0 + tanh_val)
    gelu_slope = 0.5 * (1.0 + tanh_val) + 0.5 * pre_act * (
        1.0 - tanh_val * tanh_val
    ) * gelu_scale * (1.0 + 0.134145 * pre_act * pre_act)
    return (activation, gelu_slope)


def shards(tokens, grad_out, input_weight_blocks, output_weight_blocks, row_ids, lengths):
    tok_rows = tokens.shape[0]
    groups = input_weight_blocks.shape[0] // BLOCKS_PER_COLUMN
    live_rows = lax.iota(jnp.int32, tok_rows)[:, None] < lengths[0]
    masked = jnp.where(live_rows, grad_out, jnp.zeros_like(grad_out))
    features = lax.all_gather(tokens, "blk", axis=1, tiled=True)
    x_slots = features.reshape(tok_rows, -1, BLOCK_SIDE)[:, row_ids, :]
    pre_slot = jnp.einsum(
        "tkc,kch->tkh", x_slots, input_weight_blocks, preferred_element_type=jnp.float32
    )
    pre_act = pre_slot.reshape(tok_rows, groups, BLOCKS_PER_COLUMN, BLOCK_SIDE).sum(2)
    activation, gelu_slope = gelu_pair(pre_act)
    activation = activation.astype(jnp.bfloat16)
    gradient = lax.all_gather(masked, "blk", axis=1, tiled=True)
    gradient_slots = gradient.reshape(tok_rows, -1, BLOCK_SIDE)[:, row_ids, :]
    g_four = gradient_slots.reshape(tok_rows, groups, BLOCKS_PER_COLUMN, BLOCK_SIDE)
    output_share = jnp.einsum(
        "tgh,tgrf->grhf", activation, g_four, preferred_element_type=jnp.float32
    )
    output_share = output_share.reshape(-1, BLOCK_SIDE, BLOCK_SIDE)
    slot_gradient = jnp.einsum(
        "xcn,cpn->xcp", gradient_slots, output_weight_blocks, preferred_element_type=jnp.float32
    )
    grad_act = slot_gradient.reshape(tok_rows, groups, BLOCKS_PER_COLUMN, BLOCK_SIDE).sum(2)
    grad_pre = (grad_act * gelu_slope).astype(jnp.bfloat16)
    x_four = x_slots.reshape(tok_rows, groups, BLOCKS_PER_COLUMN, BLOCK_SIDE)
    input_share = jnp.einsum("tgrc,tgh->grch", x_four, grad_pre, preferred_element_type=jnp.float32)
    input_share = input_share.reshape(-1, BLOCK_SIDE, BLOCK_SIDE)
    in_total, out_total = (
        lax.psum_scatter(
            input_share.astype(jnp.bfloat16), "seq", scatter_dimension=1, tiled=True
        ).astype(jnp.float32),
        lax.psum_scatter(
            output_share.astype(jnp.bfloat16), "seq", scatter_dimension=1, tiled=True
        ).astype(jnp.float32),
    )
    return (in_total.astype(jnp.bfloat16), out_total.astype(jnp.bfloat16))


PLAN_MESH = (8, 4)
NZ = 4
ACROSS = 3
SOLO_TOGETHER = 2
TOGETHER = 4
DELIVERY_PARTS = 4
MESH = pl.DeviceIdType.MESH


def pack_gather_grad_kernel(
    tokens_ref, grad_ref, w_in_ref, w_out_ref, ids_ref, len_ref, out_in_ref, out_out_ref,
    chip, lens, give, got, feat, w_in, w_out, part, from_core, to_x, from_x, staged,
    feat_shared, part_shared, shared_core, mid,
    load_sem, core_send, core_recv, x_send, x_recv, z_send, z_recv, y_send, y_recv,
    sum_core_send, sum_core_recv, sum_x_send, sum_x_recv, store_sem,
    sz_send, sz_recv, sy_send, sy_recv, sx_send, sx_recv, sc_send, sc_recv,
):
    rows = chip.shape[2]
    width = chip.shape[3]
    solo = feat.shape[1]
    origin = feat_shared.shape[2]
    keep = solo + origin
    spare = got.shape[1]
    per = width // BLOCK_SIDE
    n_rows = feat.shape[0] // 2
    groups = part.shape[1]
    pieces = 2 * per
    early = rows - 2 * spare
    head = 2 * early
    halves = (pl.ds(0, head), pl.ds(head, rows - head))

    blk = lax.axis_index("blk")
    seq = lax.axis_index("seq")
    z, y = blk // 2, blk % 2
    x, core = seq // 2, seq % 2
    core_dev = {"seq": seq + 1 - 2 * core}
    x_dev = {"seq": seq + 2 - 4 * x}
    y_dev = {"blk": blk + 1 - 2 * y}
    up_dev = {"blk": blk + 2}
    down_dev = {"blk": blk - 2}

    def remote(src, dst, send, recv, device):
        return pltpu.make_async_remote_copy(
            src_ref=src, dst_ref=dst, send_sem=send, recv_sem=recv,
            device_id=device, device_id_type=MESH,
        )

    barrier = pltpu.get_barrier_semaphore()
    for device in (core_dev, x_dev, y_dev):
        pl.semaphore_signal(barrier, inc=1, device_id=device, device_id_type=MESH)

    @pl.when(z > 0)
    def _():
        pl.semaphore_signal(barrier, inc=1, device_id=down_dev, device_id_type=MESH)

    @pl.when(z < NZ - 1)
    def _():
        pl.semaphore_signal(barrier, inc=1, device_id=up_dev, device_id_type=MESH)

    own_loads = [
        pltpu.make_async_copy(ref, chip.at[a, core], load_sem.at[a])
        for a, ref in enumerate((tokens_ref, grad_ref))
    ]
    weight_loads = [
        pltpu.make_async_copy(w_in_ref, w_in, load_sem.at[2]),
        pltpu.make_async_copy(w_out_ref, w_out, load_sem.at[3]),
    ]
    for load in own_loads:
        load.start()
    lens[core] = jnp.full(lens.shape[1:], len_ref[0], jnp.int32)
    pl.semaphore_wait(barrier, 3 + jnp.where(z > 0, 1, 0) + jnp.where(z < NZ - 1, 1, 0))

    len_swap = remote(lens.at[core], lens.at[core], core_send.at[4], core_recv.at[4], core_dev)
    len_swap.start()
    swaps = [
        [
            remote(
                ref.at[half], chip.at[a, core, half],
                core_send.at[2 * h + a], core_recv.at[2 * h + a], core_dev,
            )
            for a, ref in enumerate((tokens_ref, grad_ref))
        ]
        for h, half in enumerate(halves)
    ]
    for swap in swaps[0] + swaps[1]:
        swap.start()
    len_swap.wait()
    len_a = lens[0][0:1, 0:1]
    len_b = lens[1][0:1, 0:1]
    count = len_a + len_b

    def places(held):
        row = lax.broadcasted_iota(jnp.int32, (1, 2 * held), 1)
        return jnp.where(
            row < held,
            jnp.where(row < len_a, row, -1),
            jnp.where(row - held < len_b, row - held + len_a, -1),
        )

    place = places(rows)
    odd_give = jnp.bitwise_and(4 * keep - count + core, 1)
    odd_got = jnp.bitwise_and(count + core, 1)
    keep_at = 2 * lax.broadcasted_iota(jnp.int32, (keep, 1), 0) + core
    give_at = 2 * keep + odd_give + 2 * lax.broadcasted_iota(jnp.int32, (spare, 1), 0)
    got_at = count + odd_got + 2 * lax.broadcasted_iota(jnp.int32, (1, spare), 1)
    one, zero = jnp.float32(1), jnp.float32(0)
    pick_early = jnp.where(places(head) == keep_at[:early], one, zero).astype(jnp.bfloat16)
    pick_late = jnp.where(place == keep_at[early:], one, zero).astype(jnp.bfloat16)
    pick_give = jnp.where(place == give_at, one, zero).astype(jnp.bfloat16)
    pick_got = jnp.where(got_at == keep_at[early:], one, zero).astype(jnp.bfloat16)

    def feat_piece(source, late, p):
        at = feat.at[(p // per) * n_rows + per * source + p % per]
        return at.at[pl.ds(early, solo - early)] if late else at.at[pl.ds(0, early)]

    def z_copy(up, source_z, other, late, p, recv_only=False):
        ref = feat_piece(2 * source_z + (1 - y if other else y), late, p)
        slot = p + (2 * pieces if other else pieces if late else 0)
        return remote(
            ref, ref, z_send.at[0 if up else 1, source_z, slot], z_recv.at[source_z, slot],
            y_dev if recv_only else (up_dev if up else down_dev),
        )

    def y_copy(source_z, source_y, late, p):
        ref = feat_piece(2 * source_z + source_y, late, p)
        slot = p + (pieces if late else 0)
        return remote(ref, ref, y_send.at[source_z, slot], y_recv.at[source_z, slot], y_dev)

    def z_both(other, late, p):
        @pl.when(z < NZ - 1)
        def _():
            z_copy(True, z, other, late, p).start()

        @pl.when(z > 0)
        def _():
            z_copy(False, z, other, late, p).start()

    def send_own(late, a):
        def body(i, carry):
            p = a * per + i
            z_both(False, late, p)
            y_copy(z, y, late, p).start()
            return carry

        lax.fori_loop(0, per, body, 0)

    def pass_on(step, late, own=True, others=True):
        below = z - 1 - step
        above = z + 1 + step

        def arrivals(other, across):
            def body(p, carry):
                @pl.when(below >= 0)
                def _():
                    z_copy(True, below, other, late, p, recv_only=True).wait_recv()

                    @pl.when(z < NZ - 1)
                    def _():
                        z_copy(True, below, other, late, p).start()

                    if not across:
                        y_copy(below, y, late, p).start()

                @pl.when(above < NZ)
                def _():
                    z_copy(False, above, other, late, p, recv_only=True).wait_recv()

                    @pl.when(z > 0)
                    def _():
                        z_copy(False, above, other, late, p).start()

                    if not across:
                        y_copy(above, y, late, p).start()

                return carry

            return body

        if late:
            lax.fori_loop(0, pieces, arrivals(False, False), 0)
        if own and not late:
            lax.fori_loop(0, ACROSS, arrivals(False, True), 0)
            lax.fori_loop(ACROSS, pieces, arrivals(False, False), 0)
        if others and not late:
            lax.fori_loop(0, ACROSS, arrivals(True, True), 0)

    def both(a):
        return chip[a].reshape(2 * rows, width)

    def place_block(block, first, a):
        block = block.astype(jnp.bfloat16)
        for i in range(per):
            feat[a * n_rows + per * blk + i, first : first + block.shape[0]] = block[
                :, i * BLOCK_SIDE : (i + 1) * BLOCK_SIDE
            ]

    def share_x(a):
        ref = feat_shared.at[pl.ds(a * n_rows + per * blk, per), x]
        return remote(ref, ref, sx_send.at[a], sx_recv.at[a], x_dev)

    def shared_piece(source, p):
        return feat_shared.at[(p // per) * n_rows + per * source + p % per]

    def shared_z(up, source_z, p, recv_only=False):
        ref = shared_piece(2 * source_z + y, p)
        return remote(
            ref, ref, sz_send.at[0 if up else 1, source_z, p], sz_recv.at[source_z, p],
            y_dev if recv_only else (up_dev if up else down_dev),
        )

    def shared_y(source_z, source_y, p):
        ref = shared_piece(2 * source_z + source_y, p)
        return remote(ref, ref, sy_send.at[source_z, p], sy_recv.at[source_z, p], y_dev)

    def send_shared(p, carry):
        shared_y(z, y, p).start()

        @pl.when(z < NZ - 1)
        def _():
            shared_z(True, z, p).start()

        @pl.when(z > 0)
        def _():
            shared_z(False, z, p).start()

        return carry

    def pass_shared(k, carry):
        step, p = k // pieces, k % pieces
        below = z - 1 - step
        above = z + 1 + step

        @pl.when(below >= 0)
        def _():
            shared_z(True, below, p, recv_only=True).wait_recv()

            @pl.when(z < NZ - 1)
            def _():
                shared_z(True, below, p).start()

            shared_y(below, y, p).start()

        @pl.when(above < NZ)
        def _():
            shared_z(False, above, p, recv_only=True).wait_recv()

            @pl.when(z > 0)
            def _():
                shared_z(False, above, p).start()

            shared_y(above, y, p).start()

        return carry

    for a in range(2):
        own_loads[a].wait()
        swaps[0][a].wait()
        heads = chip[a, :, :head].reshape(2 * head, width)
        place_block(jnp.dot(pick_early, heads, preferred_element_type=jnp.float32), 0, a)
        send_own(False, a)
    for load in weight_loads:
        load.start()
    x_moves = []
    for a in range(2):
        swaps[1][a].wait()
        give[a] = jnp.dot(pick_give, both(a), preferred_element_type=jnp.float32).astype(jnp.bfloat16)
        move = remote(give.at[a], got.at[a], x_send.at[a], x_recv.at[a], x_dev)
        move.start()
        x_moves.append(move)
    for a in range(2):
        mid[a] = jnp.dot(pick_late, both(a), preferred_element_type=jnp.float32).astype(jnp.bfloat16)

    def turn(p, carry):
        y_copy(z, 1 - y, False, p).wait_recv()
        z_both(True, False, p)
        return carry

    lax.fori_loop(0, ACROSS, turn, 0)
    pass_on(0, False)
    pass_on(1, False, others=False)
    for a in range(2):
        x_moves[a].wait()
        kept = mid[a].astype(jnp.float32) + jnp.dot(pick_got, got[a], preferred_element_type=jnp.float32)
        place_block(kept[: solo - early], early, a)
        send_own(True, a)
        last = kept[solo - early :].astype(jnp.bfloat16)
        for i in range(per):
            feat_shared[a * n_rows + per * blk + i, x] = last[
                :, i * BLOCK_SIDE : (i + 1) * BLOCK_SIDE
            ]
        share_x(a).start()
    pass_on(1, False, own=False)
    pass_on(0, True)
    pass_on(2, False)
    pass_on(1, True)
    pass_on(2, True)
    for a in range(2):
        share_x(a).wait()
    lax.fori_loop(0, pieces, send_shared, 0)

    def end_early(p, carry):
        for source_z in range(NZ):
            y_copy(source_z, 1 - y, False, p).wait_recv()
        return carry

    def end_late(p, carry):
        for source_z in range(NZ):
            y_copy(source_z, 1 - y, True, p).wait_recv()
        return carry

    lax.fori_loop(ACROSS, pieces, end_early, 0)
    lax.fori_loop(0, pieces, end_late, 0)

    for load in weight_loads:
        load.wait()

    def core_sum(g):
        return remote(
            part.at[1 - core, g], from_core.at[g], sum_core_send.at[g], sum_core_recv.at[g], core_dev
        )

    def x_sum(g):
        return remote(to_x.at[g], from_x.at[g], sum_x_send.at[g], sum_x_recv.at[g], x_dev)

    def send_sum(g):
        core_sum(g).wait_recv()
        total = part[core, g, 1 - x].astype(jnp.float32) + from_core[g, 1 - x].astype(jnp.float32)
        to_x[g] = total.astype(jnp.bfloat16)
        x_sum(g).start()

    turns = groups // TOGETHER

    def span(t):
        return pl.ds(TOGETHER * t, TOGETHER)

    quarter = BLOCK_SIDE // 4
    first = (((0,), (0,)), ((), ()))

    def column_inputs(g, rows_of):
        ids = [ids_ref[BLOCKS_PER_COLUMN * g + i] for i in range(BLOCKS_PER_COLUMN)]
        x_cat = jnp.concatenate([rows_of(r) for r in ids], axis=1)
        g_cat = jnp.concatenate([rows_of(n_rows + r) for r in ids], axis=1)
        slots = pl.ds(BLOCKS_PER_COLUMN * g, BLOCKS_PER_COLUMN)
        w_rows = w_in[slots].reshape(BLOCKS_PER_COLUMN * BLOCK_SIDE, BLOCK_SIDE)
        wo = w_out[slots]
        w_cols = jnp.concatenate([wo[i] for i in range(BLOCKS_PER_COLUMN)], axis=1)
        pre_act = jnp.dot(x_cat, w_rows, preferred_element_type=jnp.float32)
        grad_act = lax.dot_general(
            g_cat, w_cols, (((1,), (1,)), ((), ())), preferred_element_type=jnp.float32
        )
        return x_cat, g_cat, pre_act, grad_act

    def column_grads(store, g, x_cat, g_cat, pre_act, grad_act):
        activation, gelu_slope = gelu_pair(pre_act)
        activation = activation.astype(jnp.bfloat16)
        grad_pre = (grad_act * gelu_slope).astype(jnp.bfloat16)
        share_in = lax.dot_general(grad_pre, x_cat, first, preferred_element_type=jnp.float32)
        share_out = lax.dot_general(activation, g_cat, first, preferred_element_type=jnp.float32)
        share_in = share_in.astype(jnp.bfloat16)
        share_out = share_out.astype(jnp.bfloat16)
        for i in range(BLOCKS_PER_COLUMN):
            cols = slice(i * BLOCK_SIDE, (i + 1) * BLOCK_SIDE)
            two = (share_in[:, cols].T, share_out[:, cols])
            for a in range(2):
                for q in range(4):
                    store(q % 2, q // 2, g, a, i, two[a][q * quarter : (q + 1) * quarter])

    def columns_of(columns, rows_of, store):
        held = [column_inputs(g, rows_of) for g in columns]
        for g, values in zip(columns, held):
            column_grads(store, g, *values)

    def solo_rows(r):
        return feat[r]

    def solo_store(to_core, to_chip, g, a, i, value):
        part[to_core, g, to_chip, a, i] = value

    def shared_rows(r):
        return feat_shared[r].reshape(2 * origin, BLOCK_SIDE)

    def shared_store(to_core, to_chip, g, a, i, value):
        part_shared[to_core, to_chip, g, a, i] = value

    n_pass = (NZ - 1) * pieces

    solo_turns = groups // SOLO_TOGETHER

    def solo_columns(t, carry):
        columns = [SOLO_TOGETHER * t + u for u in range(SOLO_TOGETHER)]
        columns_of(columns, solo_rows, solo_store)
        for g in columns:
            core_sum(g).start()

        @pl.when(t > 0)
        def _():
            for g in columns:
                send_sum(g - SOLO_TOGETHER)

        lax.fori_loop(n_pass * t // solo_turns, n_pass * (t + 1) // solo_turns, pass_shared, 0)
        return carry

    lax.fori_loop(0, solo_turns, solo_columns, 0)
    for u in range(SOLO_TOGETHER):
        send_sum(groups - SOLO_TOGETHER + u)

    def end_shared(p, carry):
        for source_z in range(NZ):
            shared_y(source_z, 1 - y, p).wait_recv()
        return carry

    lax.fori_loop(0, pieces, end_shared, 0)

    def shared_sum(t):
        return remote(
            part_shared.at[1 - core, x, span(t)], shared_core.at[span(t)],
            sc_send.at[t], sc_recv.at[t], core_dev,
        )

    per_turn = TOGETHER * BLOCKS_PER_COLUMN

    def stores(t):
        at = pl.ds(per_turn * t, per_turn)
        return [
            pltpu.make_async_copy(staged.at[a, at], ref.at[at], store_sem.at[a, t])
            for a, ref in enumerate((out_in_ref, out_out_ref))
        ]

    def finish(t):
        shared_sum(t).wait_recv()
        for u in range(TOGETHER):
            x_sum(TOGETHER * t + u).wait_recv()
        total = (
            part[core, span(t), x].astype(jnp.float32)
            + from_core[span(t), x].astype(jnp.float32)
            + from_x[span(t)].astype(jnp.float32)
            + part_shared[core, x, span(t)].astype(jnp.float32)
            + shared_core[span(t)].astype(jnp.float32)
        ).astype(jnp.bfloat16)
        for u in range(TOGETHER):
            at = pl.ds(per_turn * t + u * BLOCKS_PER_COLUMN, BLOCKS_PER_COLUMN)
            for a in range(2):
                staged[a, at] = total[u, a]
        for store in stores(t):
            store.start()

    def turn_shared(t, carry):
        columns_of([TOGETHER * t + u for u in range(TOGETHER)], shared_rows, shared_store)
        shared_sum(t).start()

        @pl.when(t > 0)
        def _():
            finish(t - 1)

        return carry

    lax.fori_loop(0, turns, turn_shared, 0)
    finish(turns - 1)

    def end_sums(t, carry):
        for u in range(TOGETHER):
            core_sum(TOGETHER * t + u).wait_send()
            x_sum(TOGETHER * t + u).wait_send()
        shared_sum(t).wait_send()
        for store in stores(t):
            store.wait()
        return carry

    lax.fori_loop(0, turns, end_sums, 0)

    def end_sends(other, late, across):
        def body(p, carry):
            for source_z in range(NZ):
                if across:
                    if not other:
                        @pl.when(source_z == z)
                        def _():
                            y_copy(source_z, y, late, p).wait_send()
                else:
                    y_copy(source_z, y, late, p).wait_send()

                @pl.when(jnp.logical_and(z < NZ - 1, source_z <= z))
                def _():
                    z_copy(True, source_z, other, late, p).wait_send()

                @pl.when(jnp.logical_and(z > 0, source_z >= z))
                def _():
                    z_copy(False, source_z, other, late, p).wait_send()

            return carry

        return body

    lax.fori_loop(0, ACROSS, end_sends(False, False, True), 0)
    lax.fori_loop(ACROSS, pieces, end_sends(False, False, False), 0)
    lax.fori_loop(0, ACROSS, end_sends(True, False, True), 0)
    lax.fori_loop(0, pieces, end_sends(False, True, False), 0)

    def end_shared_sends(p, carry):
        for source_z in range(NZ):
            shared_y(source_z, y, p).wait_send()

            @pl.when(jnp.logical_and(z < NZ - 1, source_z <= z))
            def _():
                shared_z(True, source_z, p).wait_send()

            @pl.when(jnp.logical_and(z > 0, source_z >= z))
            def _():
                shared_z(False, source_z, p).wait_send()

        return carry

    lax.fori_loop(0, pieces, end_shared_sends, 0)


def deliver_kernel(in_ref, out_ref, in_final, out_final, held, sems):
    pairs = []
    for a, (source, target) in enumerate(((in_ref, in_final), (out_ref, out_final))):
        step = source.shape[0] // DELIVERY_PARTS
        for k in range(DELIVERY_PARTS):
            at = pl.ds(k * step, step)
            pairs.append((
                pltpu.make_async_copy(source.at[at], held.at[a, at], sems.at[0, a, k]),
                pltpu.make_async_copy(held.at[a, at], target.at[at], sems.at[1, a, k]),
            ))
    for load, store in pairs:
        load.start()
    for load, store in pairs:
        load.wait()
        store.start()
    for load, store in pairs:
        store.wait()


def packed_shards(tokens, grad_out, input_weight_blocks, output_weight_blocks, row_ids, lengths):
    rows, width = tokens.shape
    slots = input_weight_blocks.shape[0]
    groups = slots // BLOCKS_PER_COLUMN
    n_blk, n_seq = PLAN_MESH
    keep = rows * 5 // 8
    spare = rows - keep
    origin = keep // 5
    solo = keep - origin
    turns = groups // TOGETHER
    n_rows = n_blk * width // BLOCK_SIDE
    pieces = 2 * width // BLOCK_SIDE
    quarter = BLOCK_SIDE // n_seq
    sums = (2, BLOCKS_PER_COLUMN, quarter, BLOCK_SIDE)
    bf16 = jnp.bfloat16
    dma = pltpu.SemaphoreType.DMA
    any_spec = pl.BlockSpec(memory_space=pl.ANY)
    smem = pl.BlockSpec(memory_space=pltpu.SMEM)
    out = jax.ShapeDtypeStruct((slots, quarter, BLOCK_SIDE), bf16)
    parts = pl.pallas_call(
        pack_gather_grad_kernel,
        out_shape=(out, out),
        in_specs=[any_spec] * 4 + [smem] * 2,
        out_specs=(any_spec, any_spec),
        scratch_shapes=[
            pltpu.VMEM((2, 2, rows, width), bf16),
            pltpu.VMEM((2, 8, 128), jnp.int32),
            pltpu.VMEM((2, spare, width), bf16),
            pltpu.VMEM((2, spare, width), bf16),
            pltpu.VMEM((2 * n_rows, solo, BLOCK_SIDE), bf16),
            pltpu.VMEM((slots, BLOCK_SIDE, BLOCK_SIDE), bf16),
            pltpu.VMEM((slots, BLOCK_SIDE, BLOCK_SIDE), bf16),
            pltpu.VMEM((2, groups, 2) + sums, bf16),
            pltpu.VMEM((groups, 2) + sums, bf16),
            pltpu.VMEM((groups,) + sums, bf16),
            pltpu.VMEM((groups,) + sums, bf16),
            pltpu.VMEM((2, slots, quarter, BLOCK_SIDE), bf16),
            pltpu.VMEM((2 * n_rows, 2, origin, BLOCK_SIDE), bf16),
            pltpu.VMEM((2, 2, groups) + sums, bf16),
            pltpu.VMEM((groups,) + sums, bf16),
            pltpu.VMEM((2, spare, width), bf16),
            dma((4,)),
            dma((5,)),
            dma((5,)),
            dma((2,)),
            dma((2,)),
            dma((2, NZ, 2 * pieces + ACROSS)),
            dma((NZ, 2 * pieces + ACROSS)),
            dma((NZ, 2 * pieces)),
            dma((NZ, 2 * pieces)),
            dma((groups,)),
            dma((groups,)),
            dma((groups,)),
            dma((groups,)),
            dma((2, turns)),
            dma((2, NZ, pieces)),
            dma((NZ, pieces)),
            dma((NZ, pieces)),
            dma((NZ, pieces)),
            dma((2,)),
            dma((2,)),
            dma((turns,)),
            dma((turns,)),
        ],
        compiler_params=pltpu.CompilerParams(
            collective_id=0, has_side_effects=True, vmem_limit_bytes=60 * 1024 * 1024
        ),
    )(tokens, grad_out, input_weight_blocks, output_weight_blocks, row_ids, lengths)
    return pl.pallas_call(
        deliver_kernel,
        out_shape=(out, out),
        in_specs=[any_spec] * 2,
        out_specs=(any_spec, any_spec),
        scratch_shapes=[
            pltpu.VMEM((2, slots, quarter, BLOCK_SIDE), bf16),
            dma((2, 2, DELIVERY_PARTS)),
        ],
        compiler_params=pltpu.CompilerParams(vmem_limit_bytes=60 * 1024 * 1024),
    )(*parts)


def solution(mesh):
    return jax.shard_map(
        packed_shards if tuple(mesh.shape.values()) == PLAN_MESH else shards,
        mesh=mesh,
        in_specs=(
            P("seq", "blk"),
            P("seq", "blk"),
            P("blk", None, None),
            P("blk", None, None),
            P("blk"),
            P("seq"),
        ),
        out_specs=(P("blk", "seq", None), P("blk", "seq", None)),
        check_vma=False,
    )
```

```python
import jax
import jax.numpy as jnp
from jax import lax
from jax.experimental import pallas as pl
from jax.experimental.pallas import tpu as pltpu
from jax.sharding import PartitionSpec as P

BLOCK_SIDE = 128
BLOCKS_PER_COLUMN = 4


gelu_scale = 0.7978845608


def gelu_pair(pre_act):
    tanh_val = jnp.tanh(gelu_scale * (pre_act + 0.044715 * pre_act * pre_act * pre_act))
    activation = 0.5 * pre_act * (1.0 + tanh_val)
    gelu_slope = 0.5 * (1.0 + tanh_val) + 0.5 * pre_act * (
        1.0 - tanh_val * tanh_val
    ) * gelu_scale * (1.0 + 0.134145 * pre_act * pre_act)
    return (activation, gelu_slope)


def shards(tokens, grad_out, input_weight_blocks, output_weight_blocks, row_ids, lengths):
    tok_rows = tokens.shape[0]
    groups = input_weight_blocks.shape[0] // BLOCKS_PER_COLUMN
    live_rows = lax.iota(jnp.int32, tok_rows)[:, None] < lengths[0]
    masked = jnp.where(live_rows, grad_out, jnp.zeros_like(grad_out))
    features = lax.all_gather(tokens, "blk", axis=1, tiled=True)
    x_slots = features.reshape(tok_rows, -1, BLOCK_SIDE)[:, row_ids, :]
    pre_slot = jnp.einsum(
        "tkc,kch->tkh", x_slots, input_weight_blocks, preferred_element_type=jnp.float32
    )
    pre_act = pre_slot.reshape(tok_rows, groups, BLOCKS_PER_COLUMN, BLOCK_SIDE).sum(2)
    activation, gelu_slope = gelu_pair(pre_act)
    activation = activation.astype(jnp.bfloat16)
    gradient = lax.all_gather(masked, "blk", axis=1, tiled=True)
    gradient_slots = gradient.reshape(tok_rows, -1, BLOCK_SIDE)[:, row_ids, :]
    g_four = gradient_slots.reshape(tok_rows, groups, BLOCKS_PER_COLUMN, BLOCK_SIDE)
    output_share = jnp.einsum(
        "tgh,tgrf->grhf", activation, g_four, preferred_element_type=jnp.float32
    )
    output_share = output_share.reshape(-1, BLOCK_SIDE, BLOCK_SIDE)
    slot_gradient = jnp.einsum(
        "xcn,cpn->xcp", gradient_slots, output_weight_blocks, preferred_element_type=jnp.float32
    )
    grad_act = slot_gradient.reshape(tok_rows, groups, BLOCKS_PER_COLUMN, BLOCK_SIDE).sum(2)
    grad_pre = (grad_act * gelu_slope).astype(jnp.bfloat16)
    x_four = x_slots.reshape(tok_rows, groups, BLOCKS_PER_COLUMN, BLOCK_SIDE)
    input_share = jnp.einsum("tgrc,tgh->grch", x_four, grad_pre, preferred_element_type=jnp.float32)
    input_share = input_share.reshape(-1, BLOCK_SIDE, BLOCK_SIDE)
    in_total, out_total = (
        lax.psum_scatter(
            input_share.astype(jnp.bfloat16), "seq", scatter_dimension=1, tiled=True
        ).astype(jnp.float32),
        lax.psum_scatter(
            output_share.astype(jnp.bfloat16), "seq", scatter_dimension=1, tiled=True
        ).astype(jnp.float32),
    )
    return (in_total.astype(jnp.bfloat16), out_total.astype(jnp.bfloat16))


PLAN_MESH = (8, 4)
NZ = 4
ACROSS = 3
SOLO_TOGETHER = 2
TOGETHER = 4
DELIVERY_PARTS = 4
MESH = pl.DeviceIdType.MESH


def pack_gather_grad_kernel(
    tokens_ref, grad_ref, w_in_ref, w_out_ref, ids_ref, len_ref, out_in_ref, out_out_ref,
    chip, lens, give, got, feat, w_in, w_out, part, from_core, to_x, from_x, staged,
    feat_shared, part_shared, shared_core, mid,
    load_sem, core_send, core_recv, x_send, x_recv, z_send, z_recv, y_send, y_recv,
    sum_core_send, sum_core_recv, sum_x_send, sum_x_recv, store_sem,
    sz_send, sz_recv, sy_send, sy_recv, sx_send, sx_recv, sc_send, sc_recv,
):
    rows = chip.shape[2]
    width = chip.shape[3]
    solo = feat.shape[1]
    origin = feat_shared.shape[2]
    keep = solo + origin
    spare = got.shape[1]
    per = width // BLOCK_SIDE
    n_rows = feat.shape[0] // 2
    groups = part.shape[1]
    pieces = 2 * per
    early = rows - 2 * spare
    head = 2 * early
    halves = (pl.ds(0, head), pl.ds(head, rows - head))

    blk = lax.axis_index("blk")
    seq = lax.axis_index("seq")
    z, y = blk // 2, blk % 2
    x, core = seq // 2, seq % 2
    core_dev = {"seq": seq + 1 - 2 * core}
    x_dev = {"seq": seq + 2 - 4 * x}
    y_dev = {"blk": blk + 1 - 2 * y}
    up_dev = {"blk": blk + 2}
    down_dev = {"blk": blk - 2}

    def remote(src, dst, send, recv, device):
        return pltpu.make_async_remote_copy(
            src_ref=src, dst_ref=dst, send_sem=send, recv_sem=recv,
            device_id=device, device_id_type=MESH,
        )

    barrier = pltpu.get_barrier_semaphore()
    for device in (core_dev, x_dev, y_dev):
        pl.semaphore_signal(barrier, inc=1, device_id=device, device_id_type=MESH)

    @pl.when(z > 0)
    def _():
        pl.semaphore_signal(barrier, inc=1, device_id=down_dev, device_id_type=MESH)

    @pl.when(z < NZ - 1)
    def _():
        pl.semaphore_signal(barrier, inc=1, device_id=up_dev, device_id_type=MESH)

    own_loads = [
        pltpu.make_async_copy(ref, chip.at[a, core], load_sem.at[a])
        for a, ref in enumerate((tokens_ref, grad_ref))
    ]
    weight_loads = [
        pltpu.make_async_copy(w_in_ref, w_in, load_sem.at[2]),
        pltpu.make_async_copy(w_out_ref, w_out, load_sem.at[3]),
    ]
    for load in own_loads:
        load.start()
    lens[core] = jnp.full(lens.shape[1:], len_ref[0], jnp.int32)
    pl.semaphore_wait(barrier, 3 + jnp.where(z > 0, 1, 0) + jnp.where(z < NZ - 1, 1, 0))

    len_swap = remote(lens.at[core], lens.at[core], core_send.at[4], core_recv.at[4], core_dev)
    len_swap.start()
    swaps = [
        [
            remote(
                ref.at[half], chip.at[a, core, half],
                core_send.at[2 * h + a], core_recv.at[2 * h + a], core_dev,
            )
            for a, ref in enumerate((tokens_ref, grad_ref))
        ]
        for h, half in enumerate(halves)
    ]
    for swap in swaps[0] + swaps[1]:
        swap.start()
    len_swap.wait()
    len_a = lens[0][0:1, 0:1]
    len_b = lens[1][0:1, 0:1]
    count = len_a + len_b

    def places(held):
        row = lax.broadcasted_iota(jnp.int32, (1, 2 * held), 1)
        return jnp.where(
            row < held,
            jnp.where(row < len_a, row, -1),
            jnp.where(row - held < len_b, row - held + len_a, -1),
        )

    place = places(rows)
    odd_give = jnp.bitwise_and(4 * keep - count + core, 1)
    odd_got = jnp.bitwise_and(count + core, 1)
    keep_at = 2 * lax.broadcasted_iota(jnp.int32, (keep, 1), 0) + core
    give_at = 2 * keep + odd_give + 2 * lax.broadcasted_iota(jnp.int32, (spare, 1), 0)
    got_at = count + odd_got + 2 * lax.broadcasted_iota(jnp.int32, (1, spare), 1)
    one, zero = jnp.float32(1), jnp.float32(0)
    pick_early = jnp.where(places(head) == keep_at[:early], one, zero).astype(jnp.bfloat16)
    pick_late = jnp.where(place == keep_at[early:], one, zero).astype(jnp.bfloat16)
    pick_give = jnp.where(place == give_at, one, zero).astype(jnp.bfloat16)
    pick_got = jnp.where(got_at == keep_at[early:], one, zero).astype(jnp.bfloat16)

    def feat_piece(source, late, p):
        at = feat.at[(p // per) * n_rows + per * source + p % per]
        return at.at[pl.ds(early, solo - early)] if late else at.at[pl.ds(0, early)]

    def z_copy(up, source_z, other, late, p, recv_only=False):
        ref = feat_piece(2 * source_z + (1 - y if other else y), late, p)
        slot = p + (2 * pieces if other else pieces if late else 0)
        return remote(
            ref, ref, z_send.at[0 if up else 1, source_z, slot], z_recv.at[source_z, slot],
            y_dev if recv_only else (up_dev if up else down_dev),
        )

    def y_copy(source_z, source_y, late, p):
        ref = feat_piece(2 * source_z + source_y, late, p)
        slot = p + (pieces if late else 0)
        return remote(ref, ref, y_send.at[source_z, slot], y_recv.at[source_z, slot], y_dev)

    def z_both(other, late, p):
        @pl.when(z < NZ - 1)
        def _():
            z_copy(True, z, other, late, p).start()

        @pl.when(z > 0)
        def _():
            z_copy(False, z, other, late, p).start()

    def send_own(late, a):
        def body(i, carry):
            p = a * per + i
            z_both(False, late, p)
            y_copy(z, y, late, p).start()
            return carry

        lax.fori_loop(0, per, body, 0)

    def pass_on(step, late, own=True, others=True):
        below = z - 1 - step
        above = z + 1 + step

        def arrivals(other, across):
            def body(p, carry):
                @pl.when(below >= 0)
                def _():
                    z_copy(True, below, other, late, p, recv_only=True).wait_recv()

                    @pl.when(z < NZ - 1)
                    def _():
                        z_copy(True, below, other, late, p).start()

                    if not across:
                        y_copy(below, y, late, p).start()

                @pl.when(above < NZ)
                def _():
                    z_copy(False, above, other, late, p, recv_only=True).wait_recv()

                    @pl.when(z > 0)
                    def _():
                        z_copy(False, above, other, late, p).start()

                    if not across:
                        y_copy(above, y, late, p).start()

                return carry

            return body

        if late:
            lax.fori_loop(0, pieces, arrivals(False, False), 0)
        if own and not late:
            lax.fori_loop(0, ACROSS, arrivals(False, True), 0)
            lax.fori_loop(ACROSS, pieces, arrivals(False, False), 0)
        if others and not late:
            lax.fori_loop(0, ACROSS, arrivals(True, True), 0)

    def both(a):
        return chip[a].reshape(2 * rows, width)

    def place_block(block, first, a):
        block = block.astype(jnp.bfloat16)
        for i in range(per):
            feat[a * n_rows + per * blk + i, first : first + block.shape[0]] = block[
                :, i * BLOCK_SIDE : (i + 1) * BLOCK_SIDE
            ]

    def share_x(a):
        ref = feat_shared.at[pl.ds(a * n_rows + per * blk, per), x]
        return remote(ref, ref, sx_send.at[a], sx_recv.at[a], x_dev)

    def shared_piece(source, p):
        return feat_shared.at[(p // per) * n_rows + per * source + p % per]

    def shared_z(up, source_z, p, recv_only=False):
        ref = shared_piece(2 * source_z + y, p)
        return remote(
            ref, ref, sz_send.at[0 if up else 1, source_z, p], sz_recv.at[source_z, p],
            y_dev if recv_only else (up_dev if up else down_dev),
        )

    def shared_y(source_z, source_y, p):
        ref = shared_piece(2 * source_z + source_y, p)
        return remote(ref, ref, sy_send.at[source_z, p], sy_recv.at[source_z, p], y_dev)

    def send_shared(p, carry):
        shared_y(z, y, p).start()

        @pl.when(z < NZ - 1)
        def _():
            shared_z(True, z, p).start()

        @pl.when(z > 0)
        def _():
            shared_z(False, z, p).start()

        return carry

    def pass_shared(k, carry):
        step, p = k // pieces, k % pieces
        below = z - 1 - step
        above = z + 1 + step

        @pl.when(below >= 0)
        def _():
            shared_z(True, below, p, recv_only=True).wait_recv()

            @pl.when(z < NZ - 1)
            def _():
                shared_z(True, below, p).start()

            shared_y(below, y, p).start()

        @pl.when(above < NZ)
        def _():
            shared_z(False, above, p, recv_only=True).wait_recv()

            @pl.when(z > 0)
            def _():
                shared_z(False, above, p).start()

            shared_y(above, y, p).start()

        return carry

    for a in range(2):
        own_loads[a].wait()
        swaps[0][a].wait()
        heads = chip[a, :, :head].reshape(2 * head, width)
        place_block(jnp.dot(pick_early, heads, preferred_element_type=jnp.float32), 0, a)
        send_own(False, a)
    for load in weight_loads:
        load.start()
    x_moves = []
    for a in range(2):
        swaps[1][a].wait()
        give[a] = jnp.dot(pick_give, both(a), preferred_element_type=jnp.float32).astype(jnp.bfloat16)
        move = remote(give.at[a], got.at[a], x_send.at[a], x_recv.at[a], x_dev)
        move.start()
        x_moves.append(move)
    for a in range(2):
        mid[a] = jnp.dot(pick_late, both(a), preferred_element_type=jnp.float32).astype(jnp.bfloat16)

    def turn(p, carry):
        y_copy(z, 1 - y, False, p).wait_recv()
        z_both(True, False, p)
        return carry

    lax.fori_loop(0, ACROSS, turn, 0)
    pass_on(0, False)
    for a in range(2):
        x_moves[a].wait()
        kept = mid[a].astype(jnp.float32) + jnp.dot(pick_got, got[a], preferred_element_type=jnp.float32)
        place_block(kept[: solo - early], early, a)
        send_own(True, a)
        last = kept[solo - early :].astype(jnp.bfloat16)
        for i in range(per):
            feat_shared[a * n_rows + per * blk + i, x] = last[
                :, i * BLOCK_SIDE : (i + 1) * BLOCK_SIDE
            ]
        share_x(a).start()
    pass_on(1, False)
    pass_on(0, True)
    pass_on(2, False)
    pass_on(1, True)
    pass_on(2, True)
    for a in range(2):
        share_x(a).wait()
    lax.fori_loop(0, pieces, send_shared, 0)

    def end_early(p, carry):
        for source_z in range(NZ):
            y_copy(source_z, 1 - y, False, p).wait_recv()
        return carry

    def end_late(p, carry):
        for source_z in range(NZ):
            y_copy(source_z, 1 - y, True, p).wait_recv()
        return carry

    lax.fori_loop(ACROSS, pieces, end_early, 0)
    lax.fori_loop(0, pieces, end_late, 0)

    for load in weight_loads:
        load.wait()

    def core_sum(g):
        return remote(
            part.at[1 - core, g], from_core.at[g], sum_core_send.at[g], sum_core_recv.at[g], core_dev
        )

    def x_sum(g):
        return remote(to_x.at[g], from_x.at[g], sum_x_send.at[g], sum_x_recv.at[g], x_dev)

    def send_sum(g):
        core_sum(g).wait_recv()
        total = part[core, g, 1 - x].astype(jnp.float32) + from_core[g, 1 - x].astype(jnp.float32)
        to_x[g] = total.astype(jnp.bfloat16)
        x_sum(g).start()

    turns = groups // TOGETHER

    def span(t):
        return pl.ds(TOGETHER * t, TOGETHER)

    quarter = BLOCK_SIDE // 4
    first = (((0,), (0,)), ((), ()))

    def column_inputs(g, rows_of):
        ids = [ids_ref[BLOCKS_PER_COLUMN * g + i] for i in range(BLOCKS_PER_COLUMN)]
        x_cat = jnp.concatenate([rows_of(r) for r in ids], axis=1)
        g_cat = jnp.concatenate([rows_of(n_rows + r) for r in ids], axis=1)
        slots = pl.ds(BLOCKS_PER_COLUMN * g, BLOCKS_PER_COLUMN)
        w_rows = w_in[slots].reshape(BLOCKS_PER_COLUMN * BLOCK_SIDE, BLOCK_SIDE)
        wo = w_out[slots]
        w_cols = jnp.concatenate([wo[i] for i in range(BLOCKS_PER_COLUMN)], axis=1)
        pre_act = jnp.dot(x_cat, w_rows, preferred_element_type=jnp.float32)
        grad_act = lax.dot_general(
            g_cat, w_cols, (((1,), (1,)), ((), ())), preferred_element_type=jnp.float32
        )
        return x_cat, g_cat, pre_act, grad_act

    def column_grads(store, g, x_cat, g_cat, pre_act, grad_act):
        activation, gelu_slope = gelu_pair(pre_act)
        activation = activation.astype(jnp.bfloat16)
        grad_pre = (grad_act * gelu_slope).astype(jnp.bfloat16)
        share_in = lax.dot_general(grad_pre, x_cat, first, preferred_element_type=jnp.float32)
        share_out = lax.dot_general(activation, g_cat, first, preferred_element_type=jnp.float32)
        share_in = share_in.astype(jnp.bfloat16)
        share_out = share_out.astype(jnp.bfloat16)
        for i in range(BLOCKS_PER_COLUMN):
            cols = slice(i * BLOCK_SIDE, (i + 1) * BLOCK_SIDE)
            two = (share_in[:, cols].T, share_out[:, cols])
            for a in range(2):
                for q in range(4):
                    store(q % 2, q // 2, g, a, i, two[a][q * quarter : (q + 1) * quarter])

    def columns_of(columns, rows_of, store):
        held = [column_inputs(g, rows_of) for g in columns]
        for g, values in zip(columns, held):
            column_grads(store, g, *values)

    def solo_rows(r):
        return feat[r]

    def solo_store(to_core, to_chip, g, a, i, value):
        part[to_core, g, to_chip, a, i] = value

    def shared_rows(r):
        return feat_shared[r].reshape(2 * origin, BLOCK_SIDE)

    def shared_store(to_core, to_chip, g, a, i, value):
        part_shared[to_core, to_chip, g, a, i] = value

    n_pass = (NZ - 1) * pieces

    solo_turns = groups // SOLO_TOGETHER

    def solo_columns(t, carry):
        columns = [SOLO_TOGETHER * t + u for u in range(SOLO_TOGETHER)]
        columns_of(columns, solo_rows, solo_store)
        for g in columns:
            core_sum(g).start()

        @pl.when(t > 0)
        def _():
            for g in columns:
                send_sum(g - SOLO_TOGETHER)

        lax.fori_loop(n_pass * t // solo_turns, n_pass * (t + 1) // solo_turns, pass_shared, 0)
        return carry

    lax.fori_loop(0, solo_turns, solo_columns, 0)
    for u in range(SOLO_TOGETHER):
        send_sum(groups - SOLO_TOGETHER + u)

    def end_shared(p, carry):
        for source_z in range(NZ):
            shared_y(source_z, 1 - y, p).wait_recv()
        return carry

    lax.fori_loop(0, pieces, end_shared, 0)

    def shared_sum(t):
        return remote(
            part_shared.at[1 - core, x, span(t)], shared_core.at[span(t)],
            sc_send.at[t], sc_recv.at[t], core_dev,
        )

    per_turn = TOGETHER * BLOCKS_PER_COLUMN

    def stores(t):
        at = pl.ds(per_turn * t, per_turn)
        return [
            pltpu.make_async_copy(staged.at[a, at], ref.at[at], store_sem.at[a, t])
            for a, ref in enumerate((out_in_ref, out_out_ref))
        ]

    def finish(t):
        shared_sum(t).wait_recv()
        for u in range(TOGETHER):
            x_sum(TOGETHER * t + u).wait_recv()
        total = (
            part[core, span(t), x].astype(jnp.float32)
            + from_core[span(t), x].astype(jnp.float32)
            + from_x[span(t)].astype(jnp.float32)
            + part_shared[core, x, span(t)].astype(jnp.float32)
            + shared_core[span(t)].astype(jnp.float32)
        ).astype(jnp.bfloat16)
        for u in range(TOGETHER):
            at = pl.ds(per_turn * t + u * BLOCKS_PER_COLUMN, BLOCKS_PER_COLUMN)
            for a in range(2):
                staged[a, at] = total[u, a]
        for store in stores(t):
            store.start()

    def turn_shared(t, carry):
        columns_of([TOGETHER * t + u for u in range(TOGETHER)], shared_rows, shared_store)
        shared_sum(t).start()

        @pl.when(t > 0)
        def _():
            finish(t - 1)

        return carry

    lax.fori_loop(0, turns, turn_shared, 0)
    finish(turns - 1)

    def end_sums(t, carry):
        for u in range(TOGETHER):
            core_sum(TOGETHER * t + u).wait_send()
            x_sum(TOGETHER * t + u).wait_send()
        shared_sum(t).wait_send()
        for store in stores(t):
            store.wait()
        return carry

    lax.fori_loop(0, turns, end_sums, 0)

    def end_sends(other, late, across):
        def body(p, carry):
            for source_z in range(NZ):
                if across:
                    if not other:
                        @pl.when(source_z == z)
                        def _():
                            y_copy(source_z, y, late, p).wait_send()
                else:
                    y_copy(source_z, y, late, p).wait_send()

                @pl.when(jnp.logical_and(z < NZ - 1, source_z <= z))
                def _():
                    z_copy(True, source_z, other, late, p).wait_send()

                @pl.when(jnp.logical_and(z > 0, source_z >= z))
                def _():
                    z_copy(False, source_z, other, late, p).wait_send()

            return carry

        return body

    lax.fori_loop(0, ACROSS, end_sends(False, False, True), 0)
    lax.fori_loop(ACROSS, pieces, end_sends(False, False, False), 0)
    lax.fori_loop(0, ACROSS, end_sends(True, False, True), 0)
    lax.fori_loop(0, pieces, end_sends(False, True, False), 0)

    def end_shared_sends(p, carry):
        for source_z in range(NZ):
            shared_y(source_z, y, p).wait_send()

            @pl.when(jnp.logical_and(z < NZ - 1, source_z <= z))
            def _():
                shared_z(True, source_z, p).wait_send()

            @pl.when(jnp.logical_and(z > 0, source_z >= z))
            def _():
                shared_z(False, source_z, p).wait_send()

        return carry

    lax.fori_loop(0, pieces, end_shared_sends, 0)


def deliver_kernel(in_ref, out_ref, in_final, out_final, held, sems):
    pairs = []
    for a, (source, target) in enumerate(((in_ref, in_final), (out_ref, out_final))):
        step = source.shape[0] // DELIVERY_PARTS
        for k in range(DELIVERY_PARTS):
            at = pl.ds(k * step, step)
            pairs.append((
                pltpu.make_async_copy(source.at[at], held.at[a, at], sems.at[0, a, k]),
                pltpu.make_async_copy(held.at[a, at], target.at[at], sems.at[1, a, k]),
            ))
    for load, store in pairs:
        load.start()
    for load, store in pairs:
        load.wait()
        store.start()
    for load, store in pairs:
        store.wait()


def packed_shards(tokens, grad_out, input_weight_blocks, output_weight_blocks, row_ids, lengths):
    rows, width = tokens.shape
    slots = input_weight_blocks.shape[0]
    groups = slots // BLOCKS_PER_COLUMN
    n_blk, n_seq = PLAN_MESH
    keep = rows * 5 // 8
    spare = rows - keep
    origin = keep * 7 // 30
    solo = keep - origin
    turns = groups // TOGETHER
    n_rows = n_blk * width // BLOCK_SIDE
    pieces = 2 * width // BLOCK_SIDE
    quarter = BLOCK_SIDE // n_seq
    sums = (2, BLOCKS_PER_COLUMN, quarter, BLOCK_SIDE)
    bf16 = jnp.bfloat16
    dma = pltpu.SemaphoreType.DMA
    any_spec = pl.BlockSpec(memory_space=pl.ANY)
    smem = pl.BlockSpec(memory_space=pltpu.SMEM)
    out = jax.ShapeDtypeStruct((slots, quarter, BLOCK_SIDE), bf16)
    parts = pl.pallas_call(
        pack_gather_grad_kernel,
        out_shape=(out, out),
        in_specs=[any_spec] * 4 + [smem] * 2,
        out_specs=(any_spec, any_spec),
        scratch_shapes=[
            pltpu.VMEM((2, 2, rows, width), bf16),
            pltpu.VMEM((2, 8, 128), jnp.int32),
            pltpu.VMEM((2, spare, width), bf16),
            pltpu.VMEM((2, spare, width), bf16),
            pltpu.VMEM((2 * n_rows, solo, BLOCK_SIDE), bf16),
            pltpu.VMEM((slots, BLOCK_SIDE, BLOCK_SIDE), bf16),
            pltpu.VMEM((slots, BLOCK_SIDE, BLOCK_SIDE), bf16),
            pltpu.VMEM((2, groups, 2) + sums, bf16),
            pltpu.VMEM((groups, 2) + sums, bf16),
            pltpu.VMEM((groups,) + sums, bf16),
            pltpu.VMEM((groups,) + sums, bf16),
            pltpu.VMEM((2, slots, quarter, BLOCK_SIDE), bf16),
            pltpu.VMEM((2 * n_rows, 2, origin, BLOCK_SIDE), bf16),
            pltpu.VMEM((2, 2, groups) + sums, bf16),
            pltpu.VMEM((groups,) + sums, bf16),
            pltpu.VMEM((2, spare, width), bf16),
            dma((4,)),
            dma((5,)),
            dma((5,)),
            dma((2,)),
            dma((2,)),
            dma((2, NZ, 2 * pieces + ACROSS)),
            dma((NZ, 2 * pieces + ACROSS)),
            dma((NZ, 2 * pieces)),
            dma((NZ, 2 * pieces)),
            dma((groups,)),
            dma((groups,)),
            dma((groups,)),
            dma((groups,)),
            dma((2, turns)),
            dma((2, NZ, pieces)),
            dma((NZ, pieces)),
            dma((NZ, pieces)),
            dma((NZ, pieces)),
            dma((2,)),
            dma((2,)),
            dma((turns,)),
            dma((turns,)),
        ],
        compiler_params=pltpu.CompilerParams(
            collective_id=0, has_side_effects=True, vmem_limit_bytes=60 * 1024 * 1024
        ),
    )(tokens, grad_out, input_weight_blocks, output_weight_blocks, row_ids, lengths)
    return pl.pallas_call(
        deliver_kernel,
        out_shape=(out, out),
        in_specs=[any_spec] * 2,
        out_specs=(any_spec, any_spec),
        scratch_shapes=[
            pltpu.VMEM((2, slots, quarter, BLOCK_SIDE), bf16),
            dma((2, 2, DELIVERY_PARTS)),
        ],
        compiler_params=pltpu.CompilerParams(vmem_limit_bytes=60 * 1024 * 1024),
    )(*parts)


def solution(mesh):
    return jax.shard_map(
        packed_shards if tuple(mesh.shape.values()) == PLAN_MESH else shards,
        mesh=mesh,
        in_specs=(
            P("seq", "blk"),
            P("seq", "blk"),
            P("blk", None, None),
            P("blk", None, None),
            P("blk"),
            P("seq"),
        ),
        out_specs=(P("blk", "seq", None), P("blk", "seq", None)),
        check_vma=False,
    )
```
